512 devices in a mesh: blk: 128 (over y, z_lo, x), feat: 4 (over z_hi, core).
Axes of the slice: x: 4, y: 4, z: 16 (z_hi: 2, z_lo: 8; z = z_hi * 8 + z_lo), core: 2. Of those that a mesh axis runs over, the one named last changes fastest.
Arguments:
- features: bfloat16 [131072, 512], P('blk', 'feat')
- hop_noise: bfloat16 [2, 131072, 512], P(None, 'blk', 'feat'), may hold values from -4 to 4
- encoder_weight: bfloat16 [2, 512, 512], replicated, may hold values from -0.03125 to 0.03125
- block_target: int32 [128, 40], P('blk'), may hold values from 0 to 7
- block_source: int32 [128, 40], P('blk'), may hold values from 0 to 39
- block_count: int32 [128], P('blk'), may hold values from 10 to 40
- tile_mask: int32 [128, 40, 128, 128], P('blk'), may hold values 0 or 1
Outputs:
- encoded_one: bfloat16 [131072, 512], P('blk', 'feat')
- encoded_two: bfloat16 [131072, 512], P('blk', 'feat')
The draws below stay inside these ranges and needn't reach their ends.
Inputs may be any that keep to these rules, and one draw needn't show every extreme that they name: Entries k < block_count of a partition's list are live, the others are ignored. `block_source`: window index: source partition offset index // 8 - 2, row block index % 8.
All inputs are finite; a program needn't handle non-finite values. No bound on the sum of `tile_mask` on one device may be relied on, other than what follows from the above.
Results may differ from the reference program's by a relative error of at most 0.015.
Values may be sent and summed in bfloat16 or wider, within the bound.
A program may use at most 64 MiB of HBM per device.

```python
import math
import jax
import jax.numpy as jnp
from jax import lax

F = 512
TILE = 128
TILES = 8
HALF = 2
K = 40
HOPS = 2
BLOCKS = 128
NODES = 131072


def draw_features(key, part):
    key = jax.random.fold_in(key, 5)
    first_key, second_key = jax.random.split(key, 2)
    scales = jnp.exp(jax.random.uniform(first_key, (NODES, 1), jnp.float32, math.log(0.2), math.log(3.0)))
    base = jax.random.normal(second_key, (NODES, F), jnp.float32)
    return (scales * base * F ** (-0.5)).astype(jnp.bfloat16)


def with_ends(array, own_key, least, high):
    extent = array.shape
    spot = [jax.random.randint(jax.random.fold_in(own_key, axis), (), 0, extent[axis]) for axis in range(len(extent))]
    array = array.at[tuple(spot)].set(least)
    longest = extent.index(max(extent))
    spot[longest] = (spot[longest] + 1) % extent[longest]
    return array.at[tuple(spot)].set(high)


def block_levels(rng, extent, cuts, low, top_value):
    def one(dim, blocks):
        draws = jax.random.uniform(jax.random.fold_in(jax.random.fold_in(rng, 6), dim), (blocks,), jnp.float32, low / len(cuts), top_value / len(cuts))
        return jnp.repeat(jnp.exp(draws), extent[dim] // blocks).reshape((-1,) + (1,) * (len(extent) - dim - 1))

    loudness = one(*cuts[0])
    for cut in cuts[1:]:
        loudness = loudness * one(*cut)
    return loudness


def bell_draw(key, extent, deviation, reach, pieces=(), held_as=jnp.bfloat16):
    array = jax.random.normal(key, extent, jnp.float32) * deviation
    if len(pieces) > 0:
        array = block_levels(key, extent, pieces, -0.22, 0.18) * array
    return jnp.clip(array, min=-reach, max=reach).astype(held_as)


def setup_inputs(seed: int = 0) -> dict:
    streams_of = jax.random.split(jax.random.key(seed), 8)
    features = draw_features(jax.random.fold_in(streams_of[7], 71), 0)
    hop_noise = bell_draw(streams_of[1], (HOPS, NODES, F), 0.3, 4.0, ((1, 128), (2, 4)))
    encoder_weight = bell_draw(streams_of[2], (HOPS, F, F), (64 * F) ** -0.5, 0.03125)
    block_target = with_ends(jax.random.randint(streams_of[3], (BLOCKS, K), 0, TILES), jax.random.fold_in(streams_of[3], 1), 0, TILES - 1).astype(jnp.int32)
    block_source = with_ends(jax.random.randint(streams_of[4], (BLOCKS, K), 0, (2 * HALF + 1) * TILES), jax.random.fold_in(streams_of[4], 1), 0, ((2 * HALF + 1) * TILES) - 1).astype(jnp.int32)
    block_count = with_ends(jax.random.randint(streams_of[5], (BLOCKS,), K // 4, K + 1), jax.random.fold_in(streams_of[5], 1), K // 4, K).astype(jnp.int32)
    tile_mask = with_ends((jax.random.randint(streams_of[6], (BLOCKS, K, TILE, TILE), 0, 12) < 1).astype(jnp.int32), jax.random.fold_in(streams_of[6], 1), 0, 1)
    return {"features": features, "hop_noise": hop_noise, "encoder_weight": encoder_weight, "block_target": block_target, "block_source": block_source, "block_count": block_count, "tile_mask": tile_mask}


def clip_rows(current):
    widened = current.astype(jnp.float32)
    norms = jnp.sqrt(lax.optimization_barrier(jnp.sum(widened * widened, axis=1, keepdims=True)))
    return (widened / jnp.maximum(1.0, norms)).astype(jnp.bfloat16)

def aggregate_rows(clipped, block_target, block_source, block_count, tile_mask):
    tile_rows = clipped.reshape(BLOCKS, TILES, TILE, F)
    window = jnp.concatenate([jnp.roll(tile_rows, -offset, axis=0) for offset in range(-HALF, HALF + 1)], axis=1)

    def partition_step(inputs):
        window_tiles, targets, sources, count, masks = inputs
        picked = window_tiles[sources]
        products = jnp.einsum('kij,kjf->kif', masks.astype(jnp.float32), picked.astype(jnp.float32))
        active = (jnp.arange(K) < count).astype(jnp.float32)
        routing = (targets[:, None] == jnp.arange(TILES)[None, :]).astype(jnp.float32) * active[:, None]
        return jnp.einsum('kt,kif->tif', routing, products)
    aggregated = lax.map(partition_step, (window, block_target, block_source, block_count, tile_mask))
    return aggregated.reshape(NODES, F)

def reference(features, hop_noise, encoder_weight, block_target, block_source, block_count, tile_mask):
    current = features
    results = []
    for hop_index in range(HOPS):
        clipped = clip_rows(current)
        aggregate = aggregate_rows(clipped, block_target, block_source, block_count, tile_mask)
        noisy = (aggregate + hop_noise[hop_index].astype(jnp.float32)).astype(jnp.bfloat16)
        encoded = jnp.dot(noisy, encoder_weight[hop_index], preferred_element_type=jnp.float32).astype(jnp.bfloat16)
        results.append(encoded)
        current = encoded
    return (results[0], results[1])
```

```python
import jax
import jax.numpy as jnp
from jax import lax
from jax.experimental import pallas as pl
from jax.experimental.pallas import tpu as pltpu
from jax.sharding import PartitionSpec as P

TILE = 128
TILES = 8
K = 40
Q = 4
QB = TILES // Q
N_EARLY = 4
MESH = pl.DeviceIdType.MESH
F32 = jnp.float32
BF16 = jnp.bfloat16
SRC, KEEP, LAST, HAS = 40, 80, 120, 128


def remote(src, dst, sems, index, device):
    send, recv = sems
    return pltpu.make_async_remote_copy(
        src_ref=src,
        dst_ref=dst,
        send_sem=send.at[index],
        recv_sem=recv.at[index],
        device_id=device,
        device_id_type=MESH,
    )


def kernel(
    info, feat, noise, weight, mask, out_one, out_two,
    win0, win1, masks_in, masks, weights, noises, noisy, sums, squares, scales,
    encoded, own_one, own_two, noisy_two, others,
    halo0_s, halo0_r, halo1_s, halo1_r, z_s, z_r, core_s, core_r, fwd_s, fwd_r,
    noise_s, noise_r, sq_s, sq_r, sc_s, sc_r, swap_s, swap_r, local, out_sem,
):
    parts = lax.axis_size("blk")
    b = lax.axis_index("blk")
    f = lax.axis_index("feat")
    zh = lax.div(f, 2)
    core = lax.rem(f, 2)
    fz = lax.rem(f + 2, 4)
    fc = f + 1 - 2 * core
    fd = lax.rem(fc + 2, 4)
    nxt, prv = lax.rem(b + 1, parts), lax.rem(b + parts - 1, parts)
    nxt2, prv2 = lax.rem(b + 2, parts), lax.rem(b + parts - 2, parts)
    f_nxt = jnp.where(lax.rem(b, 32) == 31, fz, f)
    f_prv = jnp.where(lax.rem(b, 32) == 0, fz, f)

    def dev(blk, col):
        return {"blk": blk, "feat": col}

    halo0, halo1 = (halo0_s, halo0_r), (halo1_s, halo1_r)
    started = []

    def go(copy):
        copy.start()
        started.append(copy)

    loads = [
        pltpu.make_async_copy(feat, win0.at[pl.ds(16, 8)], local.at[0]),
        pltpu.make_async_copy(mask, masks_in, local.at[1]),
        pltpu.make_async_copy(noise.at[0], noises.at[2], local.at[2]),
        pltpu.make_async_copy(noise.at[1], noises.at[zh], local.at[3]),
        pltpu.make_async_copy(weight, weights, local.at[4]),
    ]
    for load in loads:
        load.start()

    barrier = pltpu.get_barrier_semaphore()
    for device in (
        dev(nxt, f), dev(prv, f), dev(nxt2, f), dev(prv2, f), dev(nxt, fz), dev(prv, fz),
        dev(b, fz), dev(b, fc), dev(b, fd),
    ):
        pl.semaphore_signal(barrier, inc=1, device_id=device, device_id_type=MESH)
    pl.semaphore_wait(barrier, 9)

    def halo0_copy(way, step, q):
        to = dev(nxt, f) if way == 0 else dev(prv, f)
        here = (16, 8, 0)[step] if way == 0 else (16, 24, 32)[step]
        there = (16, 8, 0)[step + 1] if way == 0 else (16, 24, 32)[step + 1]
        src = feat.at[pl.ds(q * QB, QB)] if step == 0 else win0.at[pl.ds(here + q * QB, QB)]
        return remote(src, win0.at[pl.ds(there + q * QB, QB)], halo0, (way * 2 + step) * Q + q, to)

    for q in range(Q):
        go(halo0_copy(0, 0, q))
        go(halo0_copy(1, 0, q))

    ones = jnp.ones((8, TILE), F32)
    for t in range(TILES):
        wide = feat[t].astype(F32)
        row = lax.dot_general(
            ones, wide * wide, (((1,), (1,)), ((), ())),
            precision=lax.Precision.HIGHEST, preferred_element_type=F32,
        )
        squares[0, t : t + 1, :] = row[0:1, :]
    for i, col in enumerate((fz, fc, fd)):
        go(remote(squares.at[0], squares.at[i + 1], (sq_s, sq_r), i, dev(b, col)))

    def noise_copy(t):
        return remote(noise.at[1, t], noises.at[zh, t], (noise_s, noise_r), t, dev(b, fz))

    for t in range(N_EARLY):
        go(noise_copy(t))

    def pass_on(q):
        for way in range(2):
            halo0_copy(way, 0, q).wait_recv()
            go(halo0_copy(way, 1, q))

    pass_on(0)
    pass_on(1)

    for i, col in enumerate((fz, fc, fd)):
        remote(squares.at[0], squares.at[i + 1], (sq_s, sq_r), i, dev(b, col)).wait_recv()
    total = (squares[0] + squares[1]) + (squares[2] + squares[3])
    scales[16:24, :] = 1.0 / jnp.maximum(1.0, jnp.sqrt(total))
    scale_copies = [
        remote(scales.at[pl.ds(16, 8)], scales.at[pl.ds(there, 8)], (sc_s, sc_r), i, dev(blk, f))
        for i, (there, blk) in enumerate(((8, nxt), (0, nxt2), (24, prv), (32, prv2)))
    ]
    for copy in scale_copies:
        go(copy)
    for q in range(2, Q):
        pass_on(q)

    loads[1].wait()

    def take_mask(k, carry):
        masks[k] = masks_in[info[k]].astype(F32).astype(BF16)
        return carry

    lax.fori_loop(0, K, take_mask, 0)
    loads[0].wait()
    for copy in scale_copies:
        copy.wait_recv()
    for q in range(Q):
        for way in range(2):
            halo0_copy(way, 1, q).wait_recv()

    def add_up(width, left, right):
        def step(i, acc):
            for u in range(4):
                k = i * 4 + u
                keep = info[KEEP + k].astype(F32)
                acc = acc * keep + jnp.dot(left(k), right(k), preferred_element_type=F32)
                sums[k, :, 0:width] = acc
            return acc

        lax.fori_loop(0, K // 4, step, jnp.zeros((TILE, width), F32))

    def scaled_mask(k):
        row = scales[pl.ds(info[SRC + k], 1), :]
        return (masks[k].astype(F32) * row).astype(BF16)

    add_up(TILE, scaled_mask, lambda k: win0[info[SRC + k]])

    def z_copy(t, col):
        return remote(noisy.at[col, t], noisy.at[col, t], (z_s, z_r), t, dev(b, fz))

    def core_copy(t, col):
        return remote(noisy.at[col, t], noisy.at[col, t], (core_s, core_r), t, dev(b, fc))

    def fwd_copy(t, col):
        return remote(noisy.at[col, t], noisy.at[col, t], (fwd_s, fwd_r), t, dev(b, fc))

    loads[2].wait()
    for t in range(TILES):
        has = info[HAS + t].astype(F32)
        rows = sums[info[LAST + t], :, 0:TILE] * has
        noisy[f, t] = (rows + noises[2, t].astype(F32)).astype(BF16)
        go(z_copy(t, f))
        go(core_copy(t, f))

    loads[4].wait()

    def halo1_copy(way, step, t):
        to = dev(nxt, f_nxt) if way == 0 else dev(prv, f_prv)
        here = (16, 8, 0)[step] if way == 0 else (16, 24, 32)[step]
        there = (16, 8, 0)[step + 1] if way == 0 else (16, 24, 32)[step + 1]
        return remote(win1.at[here + t], win1.at[there + t], halo1, (way * 2 + step) * TILES + t, to)

    outs = []

    def encode(t):
        core_copy(t, fc).wait_recv()
        fwd_copy(t, fd).wait_recv()
        left = jnp.concatenate([noisy[g, t] for g in range(4)], axis=1)
        rounded = jnp.dot(left, weights[0], preferred_element_type=F32).astype(BF16)
        wide = rounded.astype(F32)
        norm = jnp.sqrt(jnp.sum(wide * wide, axis=1, keepdims=True))
        inverse = 1.0 / jnp.maximum(1.0, norm)
        for g in range(4):
            encoded[g] = rounded[:, g * TILE : (g + 1) * TILE]
        own_one[t] = encoded[f]
        for half in range(2):
            win1[16 + t, half] = (encoded[half * 2 + core].astype(F32) * inverse).astype(BF16)
        for way in range(2):
            go(halo1_copy(way, 0, t))
        copy = pltpu.make_async_copy(own_one.at[t], out_one.at[t], out_sem.at[t])
        copy.start()
        outs.append(copy)

    def pass_on_one(t):
        for way in range(2):
            halo1_copy(way, 0, t).wait_recv()
            go(halo1_copy(way, 1, t))

    for t in range(TILES + 3):
        if t < TILES:
            z_copy(t, fz).wait_recv()
            go(fwd_copy(t, fz))
        if 0 <= t - 1 < TILES:
            encode(t - 1)
        if t == 5:
            for late in range(N_EARLY, TILES):
                go(noise_copy(late))
        if 0 <= t - 3 < TILES:
            pass_on_one(t - 3)

    for t in range(TILES):
        for way in range(2):
            halo1_copy(way, 1, t).wait_recv()

    add_up(
        2 * TILE,
        lambda k: masks[k],
        lambda k: jnp.concatenate([win1[info[SRC + k], 0], win1[info[SRC + k], 1]], axis=1),
    )

    def swap_copy(t):
        return remote(noisy_two.at[t], others.at[t], (swap_s, swap_r), t, dev(b, fc))

    loads[3].wait()
    for t in range(TILES):
        remote(
            noise.at[1, t], noises.at[1 - zh, t], (noise_s, noise_r), t, dev(b, fz)
        ).wait_recv()
        has = info[HAS + t].astype(F32)
        rows = sums[info[LAST + t]] * has
        for half in range(2):
            noisy_two[t, half] = (
                rows[:, half * TILE : (half + 1) * TILE] + noises[half, t].astype(F32)
            ).astype(BF16)
        go(swap_copy(t))

    mine = pl.ds(pl.multiple_of(f * TILE, TILE), TILE)
    upper = pl.multiple_of(core * TILE, TILE)
    other = pl.multiple_of(TILE - core * TILE, TILE)
    for t in range(TILES):
        swap_copy(t).wait_recv()
        left = jnp.concatenate(
            [noisy_two[t, 0], noisy_two[t, 1], others[t, 0], others[t, 1]], axis=1
        )
        right = jnp.concatenate(
            [
                weights[1, pl.ds(upper, TILE), mine],
                weights[1, pl.ds(upper + 2 * TILE, TILE), mine],
                weights[1, pl.ds(other, TILE), mine],
                weights[1, pl.ds(other + 2 * TILE, TILE), mine],
            ],
            axis=0,
        )
        own_two[t] = jnp.dot(left, right, preferred_element_type=F32).astype(BF16)
        copy = pltpu.make_async_copy(own_two.at[t], out_two.at[t], out_sem.at[TILES + t])
        copy.start()
        outs.append(copy)

    for copy in started:
        copy.wait_send()
    for copy in outs:
        copy.wait()


def list_order(targets, sources, count):
    spots = jnp.arange(K)
    live = spots < count
    key = jnp.where(live, targets, TILES) * 64 + spots
    rank = jnp.sum(key[None, :] < key[:, None], axis=1)
    at = rank[:, None] == spots[None, :]
    perm = jnp.sum(jnp.where(at, spots[:, None], 0), axis=0)
    src = jnp.sum(jnp.where(at, sources[:, None], 0), axis=0)
    low = jnp.sum(jnp.where(at, (key // 64)[:, None], 0), axis=0)
    keep = (jnp.concatenate([jnp.full((1,), -1, low.dtype), low[:-1]]) == low).astype(jnp.int32)
    tiles = jnp.arange(TILES)
    last = jnp.maximum(jnp.sum(key[None, :] < (tiles[:, None] + 1) * 64, axis=1) - 1, 0)
    has = jnp.any((key // 64)[None, :] == tiles[:, None], axis=1)
    return jnp.concatenate([v.astype(jnp.int32) for v in (perm, src, keep, last, has)])


def per_device(
    features, hop_noise, encoder_weight, block_target, block_source, block_count, tile_mask
):
    info = list_order(block_target[0], block_source[0], block_count[0])
    tiles = (TILES, TILE, TILE)
    dma = pltpu.SemaphoreType.DMA
    anywhere = pl.BlockSpec(memory_space=pl.ANY)
    one, two = pl.pallas_call(
        kernel,
        out_shape=[jax.ShapeDtypeStruct(tiles, BF16)] * 2,
        in_specs=[
            pl.BlockSpec(memory_space=pltpu.SMEM),
            pl.BlockSpec(memory_space=pltpu.VMEM),
            anywhere, anywhere, anywhere,
        ],
        out_specs=[anywhere, anywhere],
        scratch_shapes=[
            pltpu.VMEM((K, TILE, TILE), BF16),
            pltpu.VMEM((K, 2, TILE, TILE), BF16),
            pltpu.VMEM((K, TILE, TILE), jnp.int32),
            pltpu.VMEM((K, TILE, TILE), BF16),
            pltpu.VMEM((2, 512, 512), BF16),
            pltpu.VMEM((3,) + tiles, BF16),
            pltpu.VMEM((4,) + tiles, BF16),
            pltpu.VMEM((K, TILE, 2 * TILE), F32),
            pltpu.VMEM((4, TILES, TILE), F32),
            pltpu.VMEM((K, TILE), F32),
            pltpu.VMEM((4, TILE, TILE), BF16),
            pltpu.VMEM(tiles, BF16),
            pltpu.VMEM(tiles, BF16),
            pltpu.VMEM((TILES, 2, TILE, TILE), BF16),
            pltpu.VMEM((TILES, 2, TILE, TILE), BF16),
            dma((4 * Q,)), dma((4 * Q,)),
            dma((4 * TILES,)), dma((4 * TILES,)),
            dma((TILES,)), dma((TILES,)),
            dma((TILES,)), dma((TILES,)),
            dma((TILES,)), dma((TILES,)),
            dma((TILES,)), dma((TILES,)),
            dma((3,)), dma((3,)),
            dma((4,)), dma((4,)),
            dma((TILES,)), dma((TILES,)),
            dma((5,)),
            dma((2 * TILES,)),
        ],
        compiler_params=pltpu.CompilerParams(
            collective_id=0, has_side_effects=True, vmem_limit_bytes=40 << 20
        ),
    )(
        info,
        features.reshape(tiles),
        hop_noise.reshape((2,) + tiles),
        encoder_weight,
        tile_mask[0],
    )
    return one.reshape(features.shape), two.reshape(features.shape)


def solution(mesh):
    in_specs = (
        P("blk", "feat"),
        P(None, "blk", "feat"),
        P(),
        P("blk", None),
        P("blk", None),
        P("blk"),
        P("blk", None, None, None),
    )
    out_specs = (P("blk", "feat"), P("blk", "feat"))
    return jax.shard_map(
        per_device, mesh=mesh, in_specs=in_specs, out_specs=out_specs, check_vma=False
    )
```

```python
import jax
import jax.numpy as jnp
from jax import lax
from jax.experimental import pallas as pl
from jax.experimental.pallas import tpu as pltpu
from jax.sharding import PartitionSpec as P

TILE = 128
TILES = 8
K = 40
Q = 4
QB = TILES // Q
EARLY = 3
LATE_AT = 7
WINDOW = 3
DRIP = 8
LAG = 2
MESH = pl.DeviceIdType.MESH
F32 = jnp.float32
BF16 = jnp.bfloat16
SRC, KEEP, LAST, HAS = 40, 80, 120, 128


class Links:
    def __init__(self, sems):
        self.sems = sems
        self.started = []
        self.known = {}
        self.arrived = set()

    def go(self, name, index, src, dst, device, lands=None, when=None):
        send, recv = self.sems[name]
        lands = index if lands is None else lands
        copy = pltpu.make_async_remote_copy(
            src_ref=src, dst_ref=dst, send_sem=send.at[index], recv_sem=recv.at[lands],
            device_id=device, device_id_type=MESH,
        )
        if when is None:
            copy.start()
        else:
            pl.when(when)(copy.start)
        self.started.append((copy, when, (name, index)))
        self.known[name, lands] = copy

    def sent(self, name, index):
        for i, (copy, when, at) in enumerate(self.started):
            if at == (name, index):
                copy.wait_send()
                del self.started[i]
                return

    def arrive(self, name, index):
        self.known[name, index].wait_recv()
        self.arrived.add((name, index))

    def finish(self):
        for copy, when, _ in self.started:
            if when is None:
                copy.wait_send()
            else:
                pl.when(when)(copy.wait_send)
        for at, copy in self.known.items():
            if at not in self.arrived:
                copy.wait_recv()


def kernel(
    info, feat, noise, weight, mask, out_one, out_two,
    win0, win1, masks_in, masks, weights, noises, noisy, sums, squares, chips, scales,
    encoded, own_one, own_two, noisy_two, others,
    halo0_s, halo0_r, halo1_s, halo1_r, z_s, z_r, core_s, core_r, fwd_s, fwd_r,
    noise_s, noise_r, sq_s, sq_r, sc_s, sc_r, swap_s, swap_r, local, out_sem,
):
    parts = lax.axis_size("blk")
    b = lax.axis_index("blk")
    f = lax.axis_index("feat")
    zh = lax.div(f, 2)
    core = lax.rem(f, 2)
    fz = lax.rem(f + 2, 4)
    fc = f + 1 - 2 * core
    fd = lax.rem(fc + 2, 4)
    row_at = lax.rem(b, 32)
    x = lax.rem(b, 4)
    inner = (x == 1) | (x == 2)
    low, high = x < 2, x >= 2

    def at(by):
        return lax.rem(b + by + parts, parts)

    def half_at(by):
        crosses = row_at + by >= 32 if by > 0 else row_at + by < 0
        return jnp.where(crosses, fz, f)

    def dev(blk, col):
        return {"blk": blk, "feat": col}

    links = Links({
        "halo0": (halo0_s, halo0_r), "halo1": (halo1_s, halo1_r), "z": (z_s, z_r),
        "core": (core_s, core_r), "fwd": (fwd_s, fwd_r), "noise": (noise_s, noise_r),
        "sq": (sq_s, sq_r), "sc": (sc_s, sc_r), "swap": (swap_s, swap_r),
    })
    go, arrive = links.go, links.arrive
    outs = []

    loads = [
        pltpu.make_async_copy(feat, win0.at[pl.ds(16, 8)], local.at[0]),
        pltpu.make_async_copy(mask, masks_in, local.at[1]),
        pltpu.make_async_copy(noise.at[0], noises.at[2], local.at[2]),
        pltpu.make_async_copy(noise.at[1], noises.at[zh], local.at[3]),
        pltpu.make_async_copy(weight, weights, local.at[4]),
    ]
    loaded = set()
    for copy in loads:
        copy.start()

    def load(i):
        loads[i].wait()
        loaded.add(i)

    def finish():
        links.finish()
        for i in range(5):
            if i not in loaded:
                loads[i].wait()
        for copy in outs:
            copy.wait()

    barrier = pltpu.get_barrier_semaphore()
    met = [dev(at(by), col) for by in (1, -1, 2, -2, 4, -4) for col in (f, fz)] + [dev(b, fz), dev(b, fc)]
    for device in met:
        pl.semaphore_signal(barrier, inc=1, device_id=device, device_id_type=MESH)

    ones = jnp.ones((8, TILE), F32)
    for t in range(TILES):
        wide = feat[t].astype(F32)
        row = lax.dot_general(
            ones, wide * wide, (((1,), (1,)), ((), ())),
            precision=lax.Precision.HIGHEST, preferred_element_type=F32,
        )
        squares[0, t : t + 1, :] = row[0:1, :]
    load(1)

    def take_mask(k, carry):
        masks[k] = masks_in[info[k]].astype(F32).astype(BF16)
        return carry

    lax.fori_loop(0, K, take_mask, 0)
    pl.semaphore_wait(barrier, len(met))

    class Halo:
        def __init__(self, name, WINDOW, count, size, half):
            self.name, self.window, self.count, self.size, self.half = name, WINDOW, count, size, half

        def part(self, block, q):
            return self.window.at[pl.ds(block + q * self.size, self.size)]

        def go(self, kind, q, src, slot, by, when=None):
            lands = {8: 0, 24: 1, 0: 2, 32: 3}[slot]
            go(
                self.name, kind * self.count + q, src, self.part(slot, q), dev(at(by), self.half(by)),
                lands * self.count + q, when,
            )

        def own(self, q, src=None, part=2):
            src = self.part(16, q) if src is None else src
            if part in (0, 2):
                self.go(2, q, src, 0, 2, low)
                self.go(3, q, src, 32, -2, high)
            if part in (1, 2):
                self.go(0, q, src, 8, 1)
                self.go(1, q, src, 24, -1)

        def far(self, q):
            @pl.when(low)
            def _():
                arrive(self.name, 3 * self.count + q)

            self.go(4, q, self.part(32, q), 0, 4, low)

            @pl.when(high)
            def _():
                arrive(self.name, 2 * self.count + q)

            self.go(5, q, self.part(0, q), 32, -4, high)

        def last(self, q):
            arrive(self.name, q)
            arrive(self.name, self.count + q)

            @pl.when(low)
            def _():
                arrive(self.name, 2 * self.count + q)

            @pl.when(high)
            def _():
                arrive(self.name, 3 * self.count + q)

    raw = Halo("halo0", win0, Q, QB, lambda by: f)
    clipped = Halo("halo1", win1, TILES, 1, half_at)
    go("sq", 0, squares.at[0], squares.at[1], dev(b, fc))
    for q in range(Q):
        raw.own(q, feat.at[pl.ds(q * QB, QB)], 0 if True else 2)
    arrive("sq", 0)
    mine_now = pl.ds(16, 8)
    chips[zh, mine_now, :] = squares[0] + squares[1]
    for i, by in enumerate((0, 1, -1, 2, -2)):
        there = pl.ds(16 - 8 * by, 8)
        go("sc", 2 * i, chips.at[zh, mine_now], chips.at[zh, there], dev(at(by), fz))
        if by:
            go("sc", 2 * i + 1, chips.at[zh, mine_now], chips.at[zh, there], dev(at(by), f))

    for q in range(Q):
        if True:
            raw.own(q, feat.at[pl.ds(q * QB, QB)], 1)

    def send_noise(t):
        go("noise", t, noise.at[1, t], noises.at[zh, t], dev(b, fz))

    for t in range(EARLY):
        send_noise(t)

    for q in range(Q):
        raw.far(q)
    load(0)
    for i in range(10):
        if i != 1:
            arrive("sc", i)
    scales[...] = 1.0 / jnp.maximum(1.0, jnp.sqrt(chips[0] + chips[1]))
    for q in range(Q):
        raw.last(q)

    def add_up(width, left, right):
        def step(i, acc):
            for u in range(4):
                k = i * 4 + u
                keep = info[KEEP + k].astype(F32)
                acc = acc * keep + jnp.dot(left(k), right(k), preferred_element_type=F32)
                sums[k, :, 0:width] = acc
            return acc

        lax.fori_loop(0, K // 4, step, jnp.zeros((TILE, width), F32))

    def scaled_mask(k):
        row = scales[pl.ds(info[SRC + k], 1), :]
        return (masks[k].astype(F32) * row).astype(BF16)

    add_up(TILE, scaled_mask, lambda k: win0[info[SRC + k]])

    load(2)

    def send_z(t):
        go("z", t, noisy.at[f, t], noisy.at[f, t], dev(b, fz))

    for t in range(TILES):
        has = info[HAS + t].astype(F32)
        rows = sums[info[LAST + t], :, 0:TILE] * has
        noisy[f, t] = (rows + noises[2, t].astype(F32)).astype(BF16)
        if t < WINDOW:
            send_z(t)
        go("core", t, noisy.at[f, t], noisy.at[f, t], dev(b, fc))

    load(4)

    def encode(t):
        arrive("core", t)
        arrive("fwd", t)
        left = jnp.concatenate([noisy[g, t] for g in range(4)], axis=1)
        rounded = jnp.dot(left, weights[0], preferred_element_type=F32).astype(BF16)
        wide = rounded.astype(F32)
        norm = jnp.sqrt(jnp.sum(wide * wide, axis=1, keepdims=True))
        inverse = 1.0 / jnp.maximum(1.0, norm)
        for g in range(4):
            encoded[g] = rounded[:, g * TILE : (g + 1) * TILE]
        own_one[t] = encoded[f]
        for half in range(2):
            win1[16 + t, half] = (encoded[half * 2 + core].astype(F32) * inverse).astype(BF16)
        clipped.own(t)
        copy = pltpu.make_async_copy(own_one.at[t], out_one.at[t], out_sem.at[t])
        copy.start()
        outs.append(copy)

    for t in range(TILES + LAG + 1):
        if t < TILES:
            if True and t + WINDOW < TILES:
                links.sent("z", t)
                send_z(t + WINDOW)
            arrive("z", t)
            if not True and t + WINDOW < TILES:
                send_z(t + WINDOW)
            go("fwd", t, noisy.at[fz, t], noisy.at[fz, t], dev(b, fc))
        if 0 <= t - 1 < TILES:
            encode(t - 1)
        if t >= LATE_AT:
            for late in range(EARLY + (t - LATE_AT) * DRIP, min(TILES, EARLY + (t - LATE_AT + 1) * DRIP)):
                send_noise(late)
        if 0 <= t - LAG - 1 < TILES:
            clipped.far(t - LAG - 1)

    for t in range(TILES):
        clipped.last(t)

    add_up(
        2 * TILE,
        lambda k: masks[k],
        lambda k: jnp.concatenate([win1[info[SRC + k], 0], win1[info[SRC + k], 1]], axis=1),
    )

    load(3)
    for t in range(TILES):
        arrive("noise", t)
        has = info[HAS + t].astype(F32)
        rows = sums[info[LAST + t]] * has
        for half in range(2):
            noisy_two[t, half] = (
                rows[:, half * TILE : (half + 1) * TILE] + noises[half, t].astype(F32)
            ).astype(BF16)
        go("swap", t, noisy_two.at[t], others.at[t], dev(b, fc))

    mine = pl.ds(pl.multiple_of(f * TILE, TILE), TILE)
    upper = pl.multiple_of(core * TILE, TILE)
    other = pl.multiple_of(TILE - core * TILE, TILE)
    for t in range(TILES):
        arrive("swap", t)
        left = jnp.concatenate(
            [noisy_two[t, 0], noisy_two[t, 1], others[t, 0], others[t, 1]], axis=1
        )
        right = jnp.concatenate(
            [weights[1, pl.ds(row, TILE), mine] for row in (upper, upper + 2 * TILE, other, other + 2 * TILE)],
            axis=0,
        )
        own_two[t] = jnp.dot(left, right, preferred_element_type=F32).astype(BF16)
        copy = pltpu.make_async_copy(own_two.at[t], out_two.at[t], out_sem.at[TILES + t])
        copy.start()
        outs.append(copy)
    finish()


def list_order(targets, sources, count):
    spots = jnp.arange(K)
    live = spots < count
    key = jnp.where(live, targets, TILES) * 64 + spots
    rank = jnp.sum(key[None, :] < key[:, None], axis=1)
    at = rank[:, None] == spots[None, :]
    perm = jnp.sum(jnp.where(at, spots[:, None], 0), axis=0)
    src = jnp.sum(jnp.where(at, sources[:, None], 0), axis=0)
    low = jnp.sum(jnp.where(at, (key // 64)[:, None], 0), axis=0)
    keep = (jnp.concatenate([jnp.full((1,), -1, low.dtype), low[:-1]]) == low).astype(jnp.int32)
    tiles = jnp.arange(TILES)
    last = jnp.maximum(jnp.sum(key[None, :] < (tiles[:, None] + 1) * 64, axis=1) - 1, 0)
    has = jnp.any((key // 64)[None, :] == tiles[:, None], axis=1)
    return jnp.concatenate([v.astype(jnp.int32) for v in (perm, src, keep, last, has)])


def per_device(
    features, hop_noise, encoder_weight, block_target, block_source, block_count, tile_mask
):
    info = list_order(block_target[0], block_source[0], block_count[0])
    tiles = (TILES, TILE, TILE)
    dma = pltpu.SemaphoreType.DMA
    anywhere = pl.BlockSpec(memory_space=pl.ANY)
    one, two = pl.pallas_call(
        kernel,
        out_shape=[jax.ShapeDtypeStruct(tiles, BF16)] * 2,
        in_specs=[
            pl.BlockSpec(memory_space=pltpu.SMEM),
            pl.BlockSpec(memory_space=pltpu.VMEM),
            anywhere, anywhere, anywhere,
        ],
        out_specs=[anywhere, anywhere],
        scratch_shapes=[
            pltpu.VMEM((K, TILE, TILE), BF16),
            pltpu.VMEM((K, 2, TILE, TILE), BF16),
            pltpu.VMEM((K, TILE, TILE), jnp.int32),
            pltpu.VMEM((K, TILE, TILE), BF16),
            pltpu.VMEM((2, 512, 512), BF16),
            pltpu.VMEM((3,) + tiles, BF16),
            pltpu.VMEM((4,) + tiles, BF16),
            pltpu.VMEM((K, TILE, 2 * TILE), F32),
            pltpu.VMEM((2, TILES, TILE), F32),
            pltpu.VMEM((2, K, TILE), F32),
            pltpu.VMEM((K, TILE), F32),
            pltpu.VMEM((4, TILE, TILE), BF16),
            pltpu.VMEM(tiles, BF16),
            pltpu.VMEM(tiles, BF16),
            pltpu.VMEM((TILES, 2, TILE, TILE), BF16),
            pltpu.VMEM((TILES, 2, TILE, TILE), BF16),
            dma((6 * TILES,)), dma((4 * TILES,)),
            dma((6 * TILES,)), dma((4 * TILES,)),
            dma((TILES,)), dma((TILES,)),
            dma((TILES,)), dma((TILES,)),
            dma((TILES,)), dma((TILES,)),
            dma((TILES,)), dma((TILES,)),
            dma((1,)), dma((1,)),
            dma((10,)), dma((10,)),
            dma((TILES,)), dma((TILES,)),
            dma((5,)),
            dma((2 * TILES,)),
        ],
        compiler_params=pltpu.CompilerParams(
            collective_id=0, has_side_effects=True, vmem_limit_bytes=60 << 20
        ),
    )(
        info,
        features.reshape(tiles),
        hop_noise.reshape((2,) + tiles),
        encoder_weight,
        tile_mask[0],
    )
    return one.reshape(features.shape), two.reshape(features.shape)


def solution(mesh):
    in_specs = (
        P("blk", "feat"),
        P(None, "blk", "feat"),
        P(),
        P("blk", None),
        P("blk", None),
        P("blk"),
        P("blk", None, None, None),
    )
    out_specs = (P("blk", "feat"), P("blk", "feat"))
    return jax.shard_map(
        per_device, mesh=mesh, in_specs=in_specs, out_specs=out_specs, check_vma=False
    )
```

```python
import jax
import jax.numpy as jnp
from jax import lax
from jax.experimental import pallas as pl
from jax.experimental.pallas import tpu as pltpu
from jax.sharding import PartitionSpec as P

TILE = 128
TILES = 8
K = 40
Q = 4
QB = TILES // Q
EARLY = 3
LATE_AT = 7
WINDOW = 3
DRIP = 8
MID = 0
LAG = 2
MESH = pl.DeviceIdType.MESH
F32 = jnp.float32
BF16 = jnp.bfloat16
PERM, SRC, KEEP, LAST, HAS = range(5)


class Links:
    def __init__(self, sems):
        self.sems = sems
        self.started = []
        self.known = {}
        self.arrived = set()

    def go(self, name, index, src, dst, device, lands=None, when=None):
        send, recv = self.sems[name]
        lands = index if lands is None else lands
        copy = pltpu.make_async_remote_copy(
            src_ref=src, dst_ref=dst, send_sem=send.at[index], recv_sem=recv.at[lands],
            device_id=device, device_id_type=MESH,
        )
        if when is None:
            copy.start()
        else:
            pl.when(when)(copy.start)
        self.started.append((copy, when, (name, index)))
        self.known[name, lands] = copy

    def sent(self, name, index):
        for i, (copy, when, at) in enumerate(self.started):
            if at == (name, index):
                copy.wait_send()
                del self.started[i]
                return

    def arrive(self, name, index):
        self.known[name, index].wait_recv()
        self.arrived.add((name, index))

    def finish(self):
        for copy, when, _ in self.started:
            if when is None:
                copy.wait_send()
            else:
                pl.when(when)(copy.wait_send)
        for at, copy in self.known.items():
            if at not in self.arrived:
                copy.wait_recv()


def list_order(targets, sources, count):
    spot_of = lax.broadcasted_iota(jnp.int32, (K, TILE), 0)
    lane = lax.broadcasted_iota(jnp.int32, (K, TILE), 1)
    same = spot_of == lane
    key = jnp.where(lane[:1] < count, targets, TILES) * 64 + lane[:1]

    def down(row):
        return jnp.sum(jnp.where(same, row, 0), axis=1, keepdims=True)

    def across(values, there):
        return jnp.sum(jnp.where(there, values, 0), axis=0, keepdims=True)

    key_down, source_down, target_down = down(key), down(sources), down(jnp.where(lane[:1] < count, targets, TILES))
    rank = jnp.sum(jnp.where((lane < K) & (key < key_down), 1, 0), axis=1, keepdims=True)
    at = rank == lane
    now = across(target_down, at)
    before = across(target_down, rank == lane - 1)
    keep = jnp.where((now == before) & (lane[:1] > 0), 1, 0)
    last = jnp.maximum(across(1, key_down < (lane + 1) * 64) - 1, 0)
    has = jnp.minimum(across(1, target_down == lane), 1)
    return across(spot_of, at), across(source_down, at), keep, last, has


def kernel(
    targets, sources, count, feat, noise, weight, mask, out_one, out_two,
    info, order, win0, win1, masks_in, masks, weights, noises, noisy, sums, squares, chips, scales,
    encoded, own_one, own_two, noisy_two, others, partial,
    halo0_s, halo0_r, halo1_s, halo1_r, z_s, z_r, core_s, core_r, fwd_s, fwd_r,
    noise_s, noise_r, sq_s, sq_r, sc_s, sc_r, swap_s, swap_r, local, out_sem,
):
    parts = lax.axis_size("blk")
    b = lax.axis_index("blk")
    f = lax.axis_index("feat")
    zh = lax.div(f, 2)
    core = lax.rem(f, 2)
    fz = lax.rem(f + 2, 4)
    fc = f + 1 - 2 * core
    fd = lax.rem(fc + 2, 4)
    row_at = lax.rem(b, 32)
    x = lax.rem(b, 4)
    inner = (x == 1) | (x == 2)
    low, high = x < 2, x >= 2

    def at(by):
        return lax.rem(b + by + parts, parts)

    def half_at(by):
        crosses = row_at + by >= 32 if by > 0 else row_at + by < 0
        return jnp.where(crosses, fz, f)

    def dev(blk, col):
        return {"blk": blk, "feat": col}

    links = Links({
        "halo0": (halo0_s, halo0_r), "halo1": (halo1_s, halo1_r), "z": (z_s, z_r),
        "core": (core_s, core_r), "fwd": (fwd_s, fwd_r), "noise": (noise_s, noise_r),
        "sq": (sq_s, sq_r), "sc": (sc_s, sc_r), "swap": (swap_s, swap_r),
    })
    go, arrive = links.go, links.arrive
    outs = []

    loads = [
        pltpu.make_async_copy(feat, win0.at[pl.ds(16, 8)], local.at[0]),
        pltpu.make_async_copy(mask, masks_in, local.at[1]),
        pltpu.make_async_copy(noise.at[0], noises.at[2], local.at[2]),
        pltpu.make_async_copy(noise.at[1], noises.at[zh], local.at[3]),
        pltpu.make_async_copy(weight, weights, local.at[4]),
    ]
    loaded = set()
    for copy in loads:
        copy.start()

    def load(i):
        loads[i].wait()
        loaded.add(i)

    def finish():
        links.finish()
        for i in range(5):
            if i not in loaded:
                loads[i].wait()
        for copy in outs:
            copy.wait()

    barrier = pltpu.get_barrier_semaphore()
    met = [dev(at(by), col) for by in (1, -1, 2, -2, 4, -4) for col in (f, fz)] + [dev(b, fz), dev(b, fc)]
    for device in met:
        pl.semaphore_signal(barrier, inc=1, device_id=device, device_id_type=MESH)

    ones = jnp.ones((8, TILE), F32)
    for t in range(TILES):
        wide = feat[t].astype(F32)
        row = lax.dot_general(
            ones, wide * wide, (((1,), (1,)), ((), ())),
            precision=lax.Precision.HIGHEST, preferred_element_type=F32,
        )
        squares[0, t : t + 1, :] = row[0:1, :]
    order[...] = jnp.zeros((8, TILE), jnp.int32)
    order[6:7, 0:K] = targets[...]
    order[7:8, 0:K] = sources[...]
    for i, row in enumerate(list_order(order[6:7, :], order[7:8, :], count[0])):
        order[i : i + 1, :] = row
    listed = pltpu.make_async_copy(order, info, local.at[5])
    listed.start()
    listed.wait()
    load(1)

    def take_mask(k, carry):
        masks[k] = masks_in[info[PERM, k]].astype(F32).astype(BF16)
        return carry

    lax.fori_loop(0, K, take_mask, 0)
    pl.semaphore_wait(barrier, len(met))

    class Halo:
        def __init__(self, name, WINDOW, count, size, half):
            self.name, self.window, self.count, self.size, self.half = name, WINDOW, count, size, half

        def part(self, block, q):
            return self.window.at[pl.ds(block + q * self.size, self.size)]

        def go(self, kind, q, src, slot, by, when=None):
            lands = {8: 0, 24: 1, 0: 2, 32: 3}[slot]
            go(
                self.name, kind * self.count + q, src, self.part(slot, q), dev(at(by), self.half(by)),
                lands * self.count + q, when,
            )

        def own(self, q, src=None, part=2):
            src = self.part(16, q) if src is None else src
            if part in (0, 2):
                self.go(2, q, src, 0, 2, low)
                self.go(3, q, src, 32, -2, high)
            if part in (1, 2):
                self.go(0, q, src, 8, 1)
                self.go(1, q, src, 24, -1)

        def far(self, q):
            @pl.when(low)
            def _():
                arrive(self.name, 3 * self.count + q)

            self.go(4, q, self.part(32, q), 0, 4, low)

            @pl.when(high)
            def _():
                arrive(self.name, 2 * self.count + q)

            self.go(5, q, self.part(0, q), 32, -4, high)

        def last(self, q):
            arrive(self.name, q)
            arrive(self.name, self.count + q)

            @pl.when(low)
            def _():
                arrive(self.name, 2 * self.count + q)

            @pl.when(high)
            def _():
                arrive(self.name, 3 * self.count + q)

    raw = Halo("halo0", win0, Q, QB, lambda by: f)
    clipped = Halo("halo1", win1, TILES, 1, half_at)
    go("sq", 0, squares.at[0], squares.at[1], dev(b, fc))
    for q in range(Q):
        raw.own(q, feat.at[pl.ds(q * QB, QB)], 0 if True else 2)
    arrive("sq", 0)
    mine_now = pl.ds(16, 8)
    chips[zh, mine_now, :] = squares[0] + squares[1]
    for i, by in enumerate((0, 1, -1, 2, -2)):
        there = pl.ds(16 - 8 * by, 8)
        go("sc", 2 * i, chips.at[zh, mine_now], chips.at[zh, there], dev(at(by), fz))
        if by:
            go("sc", 2 * i + 1, chips.at[zh, mine_now], chips.at[zh, there], dev(at(by), f))

    for q in range(Q):
        if True:
            raw.own(q, feat.at[pl.ds(q * QB, QB)], 1)

    def send_noise(t):
        go("noise", t, noise.at[1, t], noises.at[zh, t], dev(b, fz))

    for t in range(EARLY):
        send_noise(t)

    for q in range(Q):
        raw.far(q)
    load(0)
    for i in range(10):
        if i != 1:
            arrive("sc", i)
    scales[...] = 1.0 / jnp.maximum(1.0, jnp.sqrt(chips[0] + chips[1]))
    for q in range(Q):
        raw.last(q)

    for t in range(EARLY, EARLY + MID):
        send_noise(t)

    def add_up(width, left, right):
        def step(i, acc):
            for u in range(4):
                k = i * 4 + u
                keep = info[KEEP, k].astype(F32)
                acc = acc * keep + jnp.dot(left(k), right(k), preferred_element_type=F32)
                sums[k, :, 0:width] = acc
            return acc

        lax.fori_loop(0, K // 4, step, jnp.zeros((TILE, width), F32))

    def scaled_mask(k):
        row = scales[pl.ds(info[SRC, k], 1), :]
        return (masks[k].astype(F32) * row).astype(BF16)

    add_up(TILE, scaled_mask, lambda k: win0[info[SRC, k]])

    load(2)

    def send_z(t):
        go("z", t, noisy.at[f, t], noisy.at[f, t], dev(b, fz))

    for t in range(TILES):
        has = info[HAS, t].astype(F32)
        rows = sums[info[LAST, t], :, 0:TILE] * has
        noisy[f, t] = (rows + noises[2, t].astype(F32)).astype(BF16)
        if t < WINDOW:
            send_z(t)
        go("core", t, noisy.at[f, t], noisy.at[f, t], dev(b, fc))

    load(4)

    def encode(t):
        arrive("core", t)
        arrive("fwd", t)
        left = jnp.concatenate([noisy[g, t] for g in range(4)], axis=1)
        rounded = jnp.dot(left, weights[0], preferred_element_type=F32).astype(BF16)
        wide = rounded.astype(F32)
        norm = jnp.sqrt(jnp.sum(wide * wide, axis=1, keepdims=True))
        inverse = 1.0 / jnp.maximum(1.0, norm)
        for g in range(4):
            encoded[g] = rounded[:, g * TILE : (g + 1) * TILE]
        own_one[t] = encoded[f]
        for half in range(2):
            win1[16 + t, half] = (encoded[half * 2 + core].astype(F32) * inverse).astype(BF16)
        clipped.own(t)
        copy = pltpu.make_async_copy(own_one.at[t], out_one.at[t], out_sem.at[t])
        copy.start()
        outs.append(copy)

    for t in range(TILES + LAG + 1):
        if t < TILES:
            if True and t + WINDOW < TILES:
                links.sent("z", t)
                send_z(t + WINDOW)
            arrive("z", t)
            if not True and t + WINDOW < TILES:
                send_z(t + WINDOW)
            go("fwd", t, noisy.at[fz, t], noisy.at[fz, t], dev(b, fc))
        if 0 <= t - 1 < TILES:
            encode(t - 1)
        if t >= LATE_AT:
            sent = EARLY + MID + (t - LATE_AT) * DRIP
            for late in range(sent, min(TILES, sent + DRIP)):
                send_noise(late)
        if 0 <= t - LAG - 1 < TILES:
            clipped.far(t - LAG - 1)

    for t in range(TILES):
        clipped.last(t)

    add_up(
        2 * TILE,
        lambda k: masks[k],
        lambda k: jnp.concatenate([win1[info[SRC, k], 0], win1[info[SRC, k], 1]], axis=1),
    )

    load(3)
    mine = pl.ds(pl.multiple_of(f * TILE, TILE), TILE)
    upper = pl.multiple_of(core * TILE, TILE)
    other = pl.multiple_of(TILE - core * TILE, TILE)

    def columns_of(start):
        return jnp.concatenate([weights[1, pl.ds(row, TILE), mine] for row in (start, start + 2 * TILE)], axis=0)

    for t in range(TILES):
        arrive("noise", t)
        has = info[HAS, t].astype(F32)
        rows = sums[info[LAST, t]] * has
        for half in range(2):
            noisy_two[t, half] = (
                rows[:, half * TILE : (half + 1) * TILE] + noises[half, t].astype(F32)
            ).astype(BF16)
        go("swap", t, noisy_two.at[t], others.at[t], dev(b, fc))

    for t in range(TILES):
        left = jnp.concatenate([noisy_two[t, 0], noisy_two[t, 1]], axis=1)
        partial[t] = jnp.dot(left, columns_of(upper), preferred_element_type=F32)
    for t in range(TILES):
        arrive("swap", t)
        left = jnp.concatenate([others[t, 0], others[t, 1]], axis=1)
        rest = jnp.dot(left, columns_of(other), preferred_element_type=F32)
        own_two[t] = (partial[t] + rest).astype(BF16)
        copy = pltpu.make_async_copy(own_two.at[t], out_two.at[t], out_sem.at[TILES + t])
        copy.start()
        outs.append(copy)
    finish()


def per_device(
    features, hop_noise, encoder_weight, block_target, block_source, block_count, tile_mask
):
    tiles = (TILES, TILE, TILE)
    dma = pltpu.SemaphoreType.DMA
    anywhere = pl.BlockSpec(memory_space=pl.ANY)
    one, two = pl.pallas_call(
        kernel,
        out_shape=[jax.ShapeDtypeStruct(tiles, BF16)] * 2,
        in_specs=[
            pl.BlockSpec(memory_space=pltpu.VMEM),
            pl.BlockSpec(memory_space=pltpu.VMEM),
            pl.BlockSpec(memory_space=pltpu.SMEM),
            pl.BlockSpec(memory_space=pltpu.VMEM),
            anywhere, anywhere, anywhere,
        ],
        out_specs=[anywhere, anywhere],
        scratch_shapes=[
            pltpu.SMEM((8, TILE), jnp.int32),
            pltpu.VMEM((8, TILE), jnp.int32),
            pltpu.VMEM((K, TILE, TILE), BF16),
            pltpu.VMEM((K, 2, TILE, TILE), BF16),
            pltpu.VMEM((K, TILE, TILE), jnp.int32),
            pltpu.VMEM((K, TILE, TILE), BF16),
            pltpu.VMEM((2, 512, 512), BF16),
            pltpu.VMEM((3,) + tiles, BF16),
            pltpu.VMEM((4,) + tiles, BF16),
            pltpu.VMEM((K, TILE, 2 * TILE), F32),
            pltpu.VMEM((2, TILES, TILE), F32),
            pltpu.VMEM((2, K, TILE), F32),
            pltpu.VMEM((K, TILE), F32),
            pltpu.VMEM((4, TILE, TILE), BF16),
            pltpu.VMEM(tiles, BF16),
            pltpu.VMEM(tiles, BF16),
            pltpu.VMEM((TILES, 2, TILE, TILE), BF16),
            pltpu.VMEM((TILES, 2, TILE, TILE), BF16),
            pltpu.VMEM(tiles, F32),
            dma((6 * TILES,)), dma((4 * TILES,)),
            dma((6 * TILES,)), dma((4 * TILES,)),
            dma((TILES,)), dma((TILES,)),
            dma((TILES,)), dma((TILES,)),
            dma((TILES,)), dma((TILES,)),
            dma((TILES,)), dma((TILES,)),
            dma((1,)), dma((1,)),
            dma((10,)), dma((10,)),
            dma((TILES,)), dma((TILES,)),
            dma((6,)),
            dma((2 * TILES,)),
        ],
        compiler_params=pltpu.CompilerParams(
            collective_id=0, has_side_effects=True, vmem_limit_bytes=(53 << 20) + (256 << 10)
        ),
    )(
        block_target,
        block_source,
        block_count,
        features.reshape(tiles),
        hop_noise.reshape((2,) + tiles),
        encoder_weight,
        tile_mask[0],
    )
    return one.reshape(features.shape), two.reshape(features.shape)


def solution(mesh):
    in_specs = (
        P("blk", "feat"),
        P(None, "blk", "feat"),
        P(),
        P("blk", None),
        P("blk", None),
        P("blk"),
        P("blk", None, None, None),
    )
    out_specs = (P("blk", "feat"), P("blk", "feat"))
    return jax.shard_map(
        per_device, mesh=mesh, in_specs=in_specs, out_specs=out_specs, check_vma=False
    )
```

```python
import jax
import jax.numpy as jnp
from jax import lax
from jax.experimental import pallas as pl
from jax.experimental.pallas import tpu as pltpu
from jax.sharding import PartitionSpec as P

TILE = 128
TILES = 8
K = 40
Q = 4
QB = TILES // Q
EARLY = 3
LATE_AT = 7
WINDOW = 3
DRIP = 8
MID = 0
LAG = 2
MESH = pl.DeviceIdType.MESH
F32 = jnp.float32
BF16 = jnp.bfloat16
PERM, SRC, KEEP, LAST, HAS = range(5)


class Links:
    def __init__(self, sems):
        self.sems = sems
        self.started = []
        self.known = {}
        self.arrived = set()

    def go(self, name, index, src, dst, device, lands=None, when=None):
        send, recv = self.sems[name]
        lands = index if lands is None else lands
        copy = pltpu.make_async_remote_copy(
            src_ref=src, dst_ref=dst, send_sem=send.at[index], recv_sem=recv.at[lands],
            device_id=device, device_id_type=MESH,
        )
        if when is None:
            copy.start()
        else:
            pl.when(when)(copy.start)
        self.started.append((copy, when, (name, index)))
        self.known[name, lands] = copy

    def sent(self, name, index):
        for i, (copy, when, at) in enumerate(self.started):
            if at == (name, index):
                copy.wait_send()
                del self.started[i]
                return

    def arrive(self, name, index):
        self.known[name, index].wait_recv()
        self.arrived.add((name, index))

    def finish(self):
        for copy, when, _ in self.started:
            if when is None:
                copy.wait_send()
            else:
                pl.when(when)(copy.wait_send)
        for at, copy in self.known.items():
            if at not in self.arrived:
                copy.wait_recv()


def list_order(targets, sources, count):
    spot_of = lax.broadcasted_iota(jnp.int32, (K, TILE), 0)
    lane = lax.broadcasted_iota(jnp.int32, (K, TILE), 1)
    same = spot_of == lane
    key = jnp.where(lane[:1] < count, targets, TILES) * 64 + lane[:1]

    def down(row):
        return jnp.sum(jnp.where(same, row, 0), axis=1, keepdims=True)

    def across(values, there):
        return jnp.sum(jnp.where(there, values, 0), axis=0, keepdims=True)

    key_down, source_down, target_down = down(key), down(sources), down(jnp.where(lane[:1] < count, targets, TILES))
    rank = jnp.sum(jnp.where((lane < K) & (key < key_down), 1, 0), axis=1, keepdims=True)
    at = rank == lane
    now = across(target_down, at)
    before = across(target_down, rank == lane - 1)
    keep = jnp.where((now == before) & (lane[:1] > 0), 1, 0)
    last = jnp.maximum(across(1, key_down < (lane + 1) * 64) - 1, 0)
    has = jnp.minimum(across(1, target_down == lane), 1)
    return across(spot_of, at), across(source_down, at), keep, last, has


def kernel(
    targets, sources, count, feat, noise, weight, mask, out_one, out_two,
    info, order, win0, win1, masks_in, masks, weights, noises, noisy, sums, squares, chips, scales,
    encoded, own_one, own_two, noisy_two, others, partial,
    halo0_s, halo0_r, halo1_s, halo1_r, z_s, z_r, core_s, core_r, fwd_s, fwd_r,
    noise_s, noise_r, sq_s, sq_r, sc_s, sc_r, swap_s, swap_r, local, out_sem,
):
    parts = lax.axis_size("blk")
    b = lax.axis_index("blk")
    f = lax.axis_index("feat")
    zh = lax.div(f, 2)
    core = lax.rem(f, 2)
    fz = lax.rem(f + 2, 4)
    fc = f + 1 - 2 * core
    fd = lax.rem(fc + 2, 4)
    row_at = lax.rem(b, 32)
    x = lax.rem(b, 4)
    low, high = x < 2, x >= 2

    def at(by):
        return lax.rem(b + by + parts, parts)

    def half_at(by):
        crosses = row_at + by >= 32 if by > 0 else row_at + by < 0
        return jnp.where(crosses, fz, f)

    def dev(blk, col):
        return {"blk": blk, "feat": col}

    links = Links({
        "halo0": (halo0_s, halo0_r), "halo1": (halo1_s, halo1_r), "z": (z_s, z_r),
        "core": (core_s, core_r), "fwd": (fwd_s, fwd_r), "noise": (noise_s, noise_r),
        "sq": (sq_s, sq_r), "sc": (sc_s, sc_r), "swap": (swap_s, swap_r),
    })
    go, arrive = links.go, links.arrive
    outs = []

    loads = [
        pltpu.make_async_copy(feat, win0.at[pl.ds(16, 8)], local.at[0]),
        pltpu.make_async_copy(mask, masks_in, local.at[1]),
        pltpu.make_async_copy(noise.at[0], noises.at[2], local.at[2]),
        pltpu.make_async_copy(noise.at[1], noises.at[zh], local.at[3]),
        pltpu.make_async_copy(weight, weights, local.at[4]),
    ]
    loaded = set()
    for copy in loads:
        copy.start()

    def load(i):
        loads[i].wait()
        loaded.add(i)

    def finish():
        links.finish()
        for i in range(5):
            if i not in loaded:
                loads[i].wait()
        for copy in outs:
            copy.wait()

    barrier = pltpu.get_barrier_semaphore()
    met = [dev(at(by), col) for by in (1, -1, 2, -2, 3, -3) for col in (f, fz)] + [dev(b, fz), dev(b, fc)]
    for device in met:
        pl.semaphore_signal(barrier, inc=1, device_id=device, device_id_type=MESH)

    ones = jnp.ones((8, TILE), F32)
    for t in range(TILES):
        wide = feat[t].astype(F32)
        row = lax.dot_general(
            ones, wide * wide, (((1,), (1,)), ((), ())),
            precision=lax.Precision.HIGHEST, preferred_element_type=F32,
        )
        squares[0, t : t + 1, :] = row[0:1, :]
    order[...] = jnp.zeros((8, TILE), jnp.int32)
    order[6:7, 0:K] = targets[...]
    order[7:8, 0:K] = sources[...]
    for i, row in enumerate(list_order(order[6:7, :], order[7:8, :], count[0])):
        order[i : i + 1, :] = row
    listed = pltpu.make_async_copy(order, info, local.at[5])
    listed.start()
    listed.wait()
    load(1)

    def take_mask(k, carry):
        masks[k] = masks_in[info[PERM, k]].astype(F32).astype(BF16)
        return carry

    lax.fori_loop(0, K, take_mask, 0)
    pl.semaphore_wait(barrier, len(met))

    class Halo:
        def __init__(self, name, WINDOW, count, size, half):
            self.name, self.window, self.count, self.size, self.half = name, WINDOW, count, size, half

        def part(self, block, q):
            return self.window.at[pl.ds(block + q * self.size, self.size)]

        def go(self, kind, q, src, slot, by, when=None):
            lands = {8: 0, 24: 1, 0: 2, 32: 3}[slot]
            go(
                self.name, kind * self.count + q, src, self.part(slot, q), dev(at(by), self.half(by)),
                lands * self.count + q, when,
            )

        def own(self, q, src=None):
            src = self.part(16, q) if src is None else src
            self.go(0, q, src, 8, 1)
            self.go(1, q, src, 24, -1)

        def far(self, q):
            for kind, (below, above) in enumerate(((3, -3), (1, -1))):
                @pl.when(low)
                def _():
                    arrive(self.name, (1 - kind) * self.count + q)

                self.go(2 + kind, q, self.part((24, 8)[kind], q), 0, below, low)

                @pl.when(high)
                def _():
                    arrive(self.name, kind * self.count + q)

                self.go(4 + kind, q, self.part((8, 24)[kind], q), 32, above, high)

        def last(self, q):
            arrive(self.name, 2 * self.count + q)
            arrive(self.name, 3 * self.count + q)

    raw = Halo("halo0", win0, Q, QB, lambda by: f)
    clipped = Halo("halo1", win1, TILES, 1, half_at)
    go("sq", 0, squares.at[0], squares.at[1], dev(b, fc))
    for q in range(Q):
        raw.own(q, feat.at[pl.ds(q * QB, QB)])
    arrive("sq", 0)
    mine_now = pl.ds(16, 8)
    chips[zh, mine_now, :] = squares[0] + squares[1]
    for i, by in enumerate((0, 1, -1, 2, -2)):
        there = pl.ds(16 - 8 * by, 8)
        go("sc", 2 * i, chips.at[zh, mine_now], chips.at[zh, there], dev(at(by), fz))
        if by:
            go("sc", 2 * i + 1, chips.at[zh, mine_now], chips.at[zh, there], dev(at(by), f))

    def send_noise(t):
        go("noise", t, noise.at[1, t], noises.at[zh, t], dev(b, fz))

    for t in range(EARLY):
        send_noise(t)

    for q in range(Q):
        raw.far(q)
    load(0)
    for i in range(10):
        if i != 1:
            arrive("sc", i)
    scales[...] = 1.0 / jnp.maximum(1.0, jnp.sqrt(chips[0] + chips[1]))
    for q in range(Q):
        raw.last(q)

    for t in range(EARLY, EARLY + MID):
        send_noise(t)

    def add_up(width, left, right):
        def step(i, acc):
            for u in range(4):
                k = i * 4 + u
                keep = info[KEEP, k].astype(F32)
                acc = acc * keep + jnp.dot(left(k), right(k), preferred_element_type=F32)
                sums[k, :, 0:width] = acc
            return acc

        lax.fori_loop(0, K // 4, step, jnp.zeros((TILE, width), F32))

    def scaled_mask(k):
        row = scales[pl.ds(info[SRC, k], 1), :]
        return (masks[k].astype(F32) * row).astype(BF16)

    add_up(TILE, scaled_mask, lambda k: win0[info[SRC, k]])

    load(2)

    def send_z(t):
        go("z", t, noisy.at[f, t], noisy.at[f, t], dev(b, fz))

    for t in range(TILES):
        has = info[HAS, t].astype(F32)
        rows = sums[info[LAST, t], :, 0:TILE] * has
        noisy[f, t] = (rows + noises[2, t].astype(F32)).astype(BF16)
        if t < WINDOW:
            send_z(t)
        go("core", t, noisy.at[f, t], noisy.at[f, t], dev(b, fc))

    load(4)

    def encode(t):
        arrive("core", t)
        arrive("fwd", t)
        left = jnp.concatenate([noisy[g, t] for g in range(4)], axis=1)
        rounded = jnp.dot(left, weights[0], preferred_element_type=F32).astype(BF16)
        wide = rounded.astype(F32)
        norm = jnp.sqrt(jnp.sum(wide * wide, axis=1, keepdims=True))
        inverse = 1.0 / jnp.maximum(1.0, norm)
        for g in range(4):
            encoded[g] = rounded[:, g * TILE : (g + 1) * TILE]
        own_one[t] = encoded[f]
        for half in range(2):
            win1[16 + t, half] = (encoded[half * 2 + core].astype(F32) * inverse).astype(BF16)
        clipped.own(t)
        copy = pltpu.make_async_copy(own_one.at[t], out_one.at[t], out_sem.at[t])
        copy.start()
        outs.append(copy)

    for t in range(TILES + LAG + 1):
        if t < TILES:
            if True and t + WINDOW < TILES:
                links.sent("z", t)
                send_z(t + WINDOW)
            arrive("z", t)
            if not True and t + WINDOW < TILES:
                send_z(t + WINDOW)
            go("fwd", t, noisy.at[fz, t], noisy.at[fz, t], dev(b, fc))
        if 0 <= t - 1 < TILES:
            encode(t - 1)
        if t >= LATE_AT:
            sent = EARLY + MID + (t - LATE_AT) * DRIP
            for late in range(sent, min(TILES, sent + DRIP)):
                send_noise(late)
        if 0 <= t - LAG - 1 < TILES:
            clipped.far(t - LAG - 1)

    for t in range(TILES):
        clipped.last(t)

    add_up(
        2 * TILE,
        lambda k: masks[k],
        lambda k: jnp.concatenate([win1[info[SRC, k], 0], win1[info[SRC, k], 1]], axis=1),
    )

    load(3)
    mine = pl.ds(pl.multiple_of(f * TILE, TILE), TILE)
    upper = pl.multiple_of(core * TILE, TILE)
    other = pl.multiple_of(TILE - core * TILE, TILE)

    def columns_of(start):
        return jnp.concatenate([weights[1, pl.ds(row, TILE), mine] for row in (start, start + 2 * TILE)], axis=0)

    for t in range(TILES):
        arrive("noise", t)
        has = info[HAS, t].astype(F32)
        rows = sums[info[LAST, t]] * has
        for half in range(2):
            noisy_two[t, half] = (
                rows[:, half * TILE : (half + 1) * TILE] + noises[half, t].astype(F32)
            ).astype(BF16)
        go("swap", t, noisy_two.at[t], others.at[t], dev(b, fc))

    for t in range(TILES):
        left = jnp.concatenate([noisy_two[t, 0], noisy_two[t, 1]], axis=1)
        partial[t] = jnp.dot(left, columns_of(upper), preferred_element_type=F32)
    for t in range(TILES):
        arrive("swap", t)
        left = jnp.concatenate([others[t, 0], others[t, 1]], axis=1)
        rest = jnp.dot(left, columns_of(other), preferred_element_type=F32)
        own_two[t] = (partial[t] + rest).astype(BF16)
        copy = pltpu.make_async_copy(own_two.at[t], out_two.at[t], out_sem.at[TILES + t])
        copy.start()
        outs.append(copy)
    finish()


def per_device(
    features, hop_noise, encoder_weight, block_target, block_source, block_count, tile_mask
):
    tiles = (TILES, TILE, TILE)
    dma = pltpu.SemaphoreType.DMA
    anywhere = pl.BlockSpec(memory_space=pl.ANY)
    one, two = pl.pallas_call(
        kernel,
        out_shape=[jax.ShapeDtypeStruct(tiles, BF16)] * 2,
        in_specs=[
            pl.BlockSpec(memory_space=pltpu.VMEM),
            pl.BlockSpec(memory_space=pltpu.VMEM),
            pl.BlockSpec(memory_space=pltpu.SMEM),
            pl.BlockSpec(memory_space=pltpu.VMEM),
            anywhere, anywhere, anywhere,
        ],
        out_specs=[anywhere, anywhere],
        scratch_shapes=[
            pltpu.SMEM((8, TILE), jnp.int32),
            pltpu.VMEM((8, TILE), jnp.int32),
            pltpu.VMEM((K, TILE, TILE), BF16),
            pltpu.VMEM((K, 2, TILE, TILE), BF16),
            pltpu.VMEM((K, TILE, TILE), jnp.int32),
            pltpu.VMEM((K, TILE, TILE), BF16),
            pltpu.VMEM((2, 512, 512), BF16),
            pltpu.VMEM((3,) + tiles, BF16),
            pltpu.VMEM((4,) + tiles, BF16),
            pltpu.VMEM((K, TILE, 2 * TILE), F32),
            pltpu.VMEM((2, TILES, TILE), F32),
            pltpu.VMEM((2, K, TILE), F32),
            pltpu.VMEM((K, TILE), F32),
            pltpu.VMEM((4, TILE, TILE), BF16),
            pltpu.VMEM(tiles, BF16),
            pltpu.VMEM(tiles, BF16),
            pltpu.VMEM((TILES, 2, TILE, TILE), BF16),
            pltpu.VMEM((TILES, 2, TILE, TILE), BF16),
            pltpu.VMEM(tiles, F32),
            dma((6 * TILES,)), dma((4 * TILES,)),
            dma((6 * TILES,)), dma((4 * TILES,)),
            dma((TILES,)), dma((TILES,)),
            dma((TILES,)), dma((TILES,)),
            dma((TILES,)), dma((TILES,)),
            dma((TILES,)), dma((TILES,)),
            dma((1,)), dma((1,)),
            dma((10,)), dma((10,)),
            dma((TILES,)), dma((TILES,)),
            dma((6,)),
            dma((2 * TILES,)),
        ],
        compiler_params=pltpu.CompilerParams(
            collective_id=0, has_side_effects=True, vmem_limit_bytes=(53 << 20) + (256 << 10)
        ),
    )(
        block_target,
        block_source,
        block_count,
        features.reshape(tiles),
        hop_noise.reshape((2,) + tiles),
        encoder_weight,
        tile_mask[0],
    )
    return one.reshape(features.shape), two.reshape(features.shape)


def solution(mesh):
    in_specs = (
        P("blk", "feat"),
        P(None, "blk", "feat"),
        P(),
        P("blk", None),
        P("blk", None),
        P("blk"),
        P("blk", None, None, None),
    )
    out_specs = (P("blk", "feat"), P("blk", "feat"))
    return jax.shard_map(
        per_device, mesh=mesh, in_specs=in_specs, out_specs=out_specs, check_vma=False
    )
```

```python
import jax
import jax.numpy as jnp
from jax import lax
from jax.experimental import pallas as pl
from jax.experimental.pallas import tpu as pltpu
from jax.sharding import PartitionSpec as P

TILE = 128
TILES = 8
K = 40
Q = 4
QB = TILES // Q
EARLY = 3
LATE_AT = 7
WINDOW = 4
DRIP = 8
MID = 0
UNROLL = 10
LAG = 3
MESH = pl.DeviceIdType.MESH
F32 = jnp.float32
BF16 = jnp.bfloat16
PERM, SRC, KEEP, LAST, HAS = range(5)


class Links:
    def __init__(self, sems):
        self.sems = sems
        self.started = []
        self.known = {}
        self.arrived = set()

    def go(self, name, index, src, dst, device, lands=None, when=None):
        send, recv = self.sems[name]
        lands = index if lands is None else lands
        copy = pltpu.make_async_remote_copy(
            src_ref=src, dst_ref=dst, send_sem=send.at[index], recv_sem=recv.at[lands],
            device_id=device, device_id_type=MESH,
        )
        if when is None:
            copy.start()
        else:
            pl.when(when)(copy.start)
        self.started.append((copy, when, (name, index)))
        self.known[name, lands] = copy

    def sent(self, name, index):
        for i, (copy, when, at) in enumerate(self.started):
            if at == (name, index):
                copy.wait_send()
                del self.started[i]
                return

    def arrive(self, name, index):
        self.known[name, index].wait_recv()
        self.arrived.add((name, index))

    def finish(self):
        for copy, when, _ in self.started:
            if when is None:
                copy.wait_send()
            else:
                pl.when(when)(copy.wait_send)
        for at, copy in self.known.items():
            if at not in self.arrived:
                copy.wait_recv()


def list_order(targets, sources, count):
    spot_of = lax.broadcasted_iota(jnp.int32, (K, TILE), 0)
    lane = lax.broadcasted_iota(jnp.int32, (K, TILE), 1)
    same = spot_of == lane
    key = jnp.where(lane[:1] < count, targets, TILES) * 64 + lane[:1]

    def down(row):
        return jnp.sum(jnp.where(same, row, 0), axis=1, keepdims=True)

    def across(values, there):
        return jnp.sum(jnp.where(there, values, 0), axis=0, keepdims=True)

    key_down, source_down, target_down = down(key), down(sources), down(jnp.where(lane[:1] < count, targets, TILES))
    rank = jnp.sum(jnp.where((lane < K) & (key < key_down), 1, 0), axis=1, keepdims=True)
    at = rank == lane
    now = across(target_down, at)
    before = across(target_down, rank == lane - 1)
    keep = jnp.where((now == before) & (lane[:1] > 0), 1, 0)
    last = jnp.maximum(across(1, key_down < (lane + 1) * 64) - 1, 0)
    has = jnp.minimum(across(1, target_down == lane), 1)
    return across(spot_of, at), across(source_down, at), keep, last, has


def kernel(
    targets, sources, count, feat, noise, weight, mask, out_one, out_two,
    info, order, win0, win1, masks_in, masks, weights, noises, noisy, sums, squares, chips, scales,
    encoded, own_one, own_two, noisy_two, others, partial,
    halo0_s, halo0_r, halo1_s, halo1_r, z_s, z_r, core_s, core_r, fwd_s, fwd_r,
    noise_s, noise_r, sq_s, sq_r, sc_s, sc_r, swap_s, swap_r, local, out_sem,
):
    parts = lax.axis_size("blk")
    b = lax.axis_index("blk")
    f = lax.axis_index("feat")
    zh = lax.div(f, 2)
    core = lax.rem(f, 2)
    fz = lax.rem(f + 2, 4)
    fc = f + 1 - 2 * core
    fd = lax.rem(fc + 2, 4)
    row_at = lax.rem(b, 32)
    x = lax.rem(b, 4)
    low, high = x < 2, x >= 2

    def at(by):
        return lax.rem(b + by + parts, parts)

    def half_at(by):
        crosses = row_at + by >= 32 if by > 0 else row_at + by < 0
        return jnp.where(crosses, fz, f)

    def dev(blk, col):
        return {"blk": blk, "feat": col}

    links = Links({
        "halo0": (halo0_s, halo0_r), "halo1": (halo1_s, halo1_r), "z": (z_s, z_r),
        "core": (core_s, core_r), "fwd": (fwd_s, fwd_r), "noise": (noise_s, noise_r),
        "sq": (sq_s, sq_r), "sc": (sc_s, sc_r), "swap": (swap_s, swap_r),
    })
    go, arrive = links.go, links.arrive
    outs = []

    loads = [
        pltpu.make_async_copy(feat, win0.at[pl.ds(16, 8)], local.at[0]),
        pltpu.make_async_copy(mask, masks_in, local.at[1]),
        pltpu.make_async_copy(noise.at[0], noises.at[2], local.at[2]),
        pltpu.make_async_copy(noise.at[1], noises.at[zh], local.at[3]),
        pltpu.make_async_copy(weight, weights, local.at[4]),
    ]
    loaded = set()
    for copy in loads:
        copy.start()

    def load(i):
        loads[i].wait()
        loaded.add(i)

    def finish():
        links.finish()
        for i in range(5):
            if i not in loaded:
                loads[i].wait()
        for copy in outs:
            copy.wait()

    barrier = pltpu.get_barrier_semaphore()
    met = [dev(at(by), col) for by in (1, -1, 2, -2, 3, -3) for col in (f, fz)] + [dev(b, fz), dev(b, fc)]
    for device in met:
        pl.semaphore_signal(barrier, inc=1, device_id=device, device_id_type=MESH)

    ones = jnp.ones((8, TILE), F32)
    for t in range(TILES):
        wide = feat[t].astype(F32)
        row = lax.dot_general(
            ones, wide * wide, (((1,), (1,)), ((), ())),
            precision=lax.Precision.HIGHEST, preferred_element_type=F32,
        )
        squares[0, t : t + 1, :] = row[0:1, :]
    lanes = lax.broadcasted_iota(jnp.int32, (1, TILE), 1)
    target_row = source_row = jnp.zeros((1, TILE), jnp.int32)
    for k in range(K):
        target_row = jnp.where(lanes == k, targets[k], target_row)
        source_row = jnp.where(lanes == k, sources[k], source_row)
    order[...] = jnp.zeros((8, TILE), jnp.int32)
    for i, row in enumerate(list_order(target_row, source_row, count[0])):
        order[i : i + 1, :] = row
    listed = pltpu.make_async_copy(order, info, local.at[5])
    listed.start()
    listed.wait()
    load(1)

    def take_mask(k, carry):
        masks[k] = masks_in[info[PERM, k]].astype(F32).astype(BF16)
        return carry

    lax.fori_loop(0, K, take_mask, 0)
    pl.semaphore_wait(barrier, len(met))

    class Halo:
        def __init__(self, name, WINDOW, count, size, half):
            self.name, self.window, self.count, self.size, self.half = name, WINDOW, count, size, half

        def part(self, block, q):
            return self.window.at[pl.ds(block + q * self.size, self.size)]

        def go(self, kind, q, src, slot, by, when=None):
            lands = {8: 0, 24: 1, 0: 2, 32: 3}[slot]
            go(
                self.name, kind * self.count + q, src, self.part(slot, q), dev(at(by), self.half(by)),
                lands * self.count + q, when,
            )

        def own(self, q, src=None):
            src = self.part(16, q) if src is None else src
            self.go(0, q, src, 8, 1)
            self.go(1, q, src, 24, -1)

        def far(self, q):
            for kind, (below, above) in enumerate(((3, -3), (1, -1))):
                @pl.when(low)
                def _():
                    arrive(self.name, (1 - kind) * self.count + q)

                self.go(2 + kind, q, self.part((24, 8)[kind], q), 0, below, low)

                @pl.when(high)
                def _():
                    arrive(self.name, kind * self.count + q)

                self.go(4 + kind, q, self.part((8, 24)[kind], q), 32, above, high)

        def last(self, q):
            arrive(self.name, 2 * self.count + q)
            arrive(self.name, 3 * self.count + q)

    raw = Halo("halo0", win0, Q, QB, lambda by: f)
    clipped = Halo("halo1", win1, TILES, 1, half_at)
    go("sq", 0, squares.at[0], squares.at[1], dev(b, fc))
    for q in range(Q):
        raw.own(q, feat.at[pl.ds(q * QB, QB)])
    arrive("sq", 0)
    mine_now = pl.ds(16, 8)
    chips[zh, mine_now, :] = squares[0] + squares[1]
    for i, by in enumerate((0, 1, -1, 2, -2)):
        there = pl.ds(16 - 8 * by, 8)
        go("sc", 2 * i, chips.at[zh, mine_now], chips.at[zh, there], dev(at(by), fz))
        if by:
            go("sc", 2 * i + 1, chips.at[zh, mine_now], chips.at[zh, there], dev(at(by), f))

    def send_noise(t):
        go("noise", t, noise.at[1, t], noises.at[zh, t], dev(b, fz))

    for t in range(EARLY):
        send_noise(t)

    for q in range(Q):
        raw.far(q)
    load(0)
    for i in range(10):
        if i != 1:
            arrive("sc", i)
    scales[...] = 1.0 / jnp.maximum(1.0, jnp.sqrt(chips[0] + chips[1]))
    for q in range(Q):
        raw.last(q)

    for t in range(EARLY, EARLY + MID):
        send_noise(t)

    def add_up(width, left, right):
        def step(i, acc):
            for u in range(UNROLL):
                k = i * UNROLL + u
                keep = info[KEEP, k].astype(F32)
                acc = acc * keep + jnp.dot(left(k), right(k), preferred_element_type=F32)
                sums[k, :, 0:width] = acc
            return acc

        lax.fori_loop(0, K // UNROLL, step, jnp.zeros((TILE, width), F32))

    def scaled_mask(k):
        row = scales[pl.ds(info[SRC, k], 1), :]
        return (masks[k].astype(F32) * row).astype(BF16)

    add_up(TILE, scaled_mask, lambda k: win0[info[SRC, k]])

    load(2)

    def send_z(t):
        go("z", t, noisy.at[f, t], noisy.at[f, t], dev(b, fz))

    for t in range(TILES):
        has = info[HAS, t].astype(F32)
        rows = sums[info[LAST, t], :, 0:TILE] * has
        noisy[f, t] = (rows + noises[2, t].astype(F32)).astype(BF16)
        if t < WINDOW:
            send_z(t)
        go("core", t, noisy.at[f, t], noisy.at[f, t], dev(b, fc))

    load(4)

    def encode(t):
        arrive("core", t)
        arrive("fwd", t)
        left = jnp.concatenate([noisy[g, t] for g in range(4)], axis=1)
        rounded = jnp.dot(left, weights[0], preferred_element_type=F32).astype(BF16)
        wide = rounded.astype(F32)
        norm = jnp.sqrt(jnp.sum(wide * wide, axis=1, keepdims=True))
        inverse = 1.0 / jnp.maximum(1.0, norm)
        for g in range(4):
            encoded[g] = rounded[:, g * TILE : (g + 1) * TILE]
        own_one[t] = encoded[f]
        for half in range(2):
            win1[16 + t, half] = (encoded[half * 2 + core].astype(F32) * inverse).astype(BF16)
        clipped.own(t)
        copy = pltpu.make_async_copy(own_one.at[t], out_one.at[t], out_sem.at[t])
        copy.start()
        outs.append(copy)

    for t in range(TILES + LAG + 1):
        if t < TILES:
            if t + WINDOW < TILES:
                links.sent("z", t)
                send_z(t + WINDOW)
            arrive("z", t)
            go("fwd", t, noisy.at[fz, t], noisy.at[fz, t], dev(b, fc))
        if 0 <= t - 1 < TILES:
            encode(t - 1)
        if t >= LATE_AT:
            sent = EARLY + MID + (t - LATE_AT) * DRIP
            for late in range(sent, min(TILES, sent + DRIP)):
                send_noise(late)
        if 0 <= t - LAG - 1 < TILES:
            clipped.far(t - LAG - 1)

    for t in range(TILES):
        clipped.last(t)

    add_up(
        2 * TILE,
        lambda k: masks[k],
        lambda k: jnp.concatenate([win1[info[SRC, k], 0], win1[info[SRC, k], 1]], axis=1),
    )

    load(3)
    mine = pl.ds(pl.multiple_of(f * TILE, TILE), TILE)
    upper = pl.multiple_of(core * TILE, TILE)
    other = pl.multiple_of(TILE - core * TILE, TILE)

    def columns_of(start):
        return jnp.concatenate([weights[1, pl.ds(row, TILE), mine] for row in (start, start + 2 * TILE)], axis=0)

    for t in range(TILES):
        arrive("noise", t)
        has = info[HAS, t].astype(F32)
        rows = sums[info[LAST, t]] * has
        for half in range(2):
            noisy_two[t, half] = (
                rows[:, half * TILE : (half + 1) * TILE] + noises[half, t].astype(F32)
            ).astype(BF16)
        go("swap", t, noisy_two.at[t], others.at[t], dev(b, fc))

    for t in range(TILES):
        left = jnp.concatenate([noisy_two[t, 0], noisy_two[t, 1]], axis=1)
        partial[t] = jnp.dot(left, columns_of(upper), preferred_element_type=F32)
    for t in range(TILES):
        arrive("swap", t)
        left = jnp.concatenate([others[t, 0], others[t, 1]], axis=1)
        rest = jnp.dot(left, columns_of(other), preferred_element_type=F32)
        own_two[t] = (partial[t] + rest).astype(BF16)
        copy = pltpu.make_async_copy(own_two.at[t], out_two.at[t], out_sem.at[TILES + t])
        copy.start()
        outs.append(copy)
    finish()


def per_device(
    features, hop_noise, encoder_weight, block_target, block_source, block_count, tile_mask
):
    tiles = (TILES, TILE, TILE)
    dma = pltpu.SemaphoreType.DMA
    anywhere = pl.BlockSpec(memory_space=pl.ANY)
    one, two = pl.pallas_call(
        kernel,
        out_shape=[jax.ShapeDtypeStruct(tiles, BF16)] * 2,
        in_specs=[
            pl.BlockSpec(memory_space=pltpu.SMEM),
            pl.BlockSpec(memory_space=pltpu.SMEM),
            pl.BlockSpec(memory_space=pltpu.SMEM),
            pl.BlockSpec(memory_space=pltpu.VMEM),
            anywhere, anywhere, anywhere,
        ],
        out_specs=[anywhere, anywhere],
        scratch_shapes=[
            pltpu.SMEM((8, TILE), jnp.int32),
            pltpu.VMEM((8, TILE), jnp.int32),
            pltpu.VMEM((K, TILE, TILE), BF16),
            pltpu.VMEM((K, 2, TILE, TILE), BF16),
            pltpu.VMEM((K, TILE, TILE), jnp.int32),
            pltpu.VMEM((K, TILE, TILE), BF16),
            pltpu.VMEM((2, 512, 512), BF16),
            pltpu.VMEM((3,) + tiles, BF16),
            pltpu.VMEM((4,) + tiles, BF16),
            pltpu.VMEM((K, TILE, 2 * TILE), F32),
            pltpu.VMEM((2, TILES, TILE), F32),
            pltpu.VMEM((2, K, TILE), F32),
            pltpu.VMEM((K, TILE), F32),
            pltpu.VMEM((4, TILE, TILE), BF16),
            pltpu.VMEM(tiles, BF16),
            pltpu.VMEM(tiles, BF16),
            pltpu.VMEM((TILES, 2, TILE, TILE), BF16),
            pltpu.VMEM((TILES, 2, TILE, TILE), BF16),
            pltpu.VMEM(tiles, F32),
            dma((6 * TILES,)), dma((4 * TILES,)),
            dma((6 * TILES,)), dma((4 * TILES,)),
            dma((TILES,)), dma((TILES,)),
            dma((TILES,)), dma((TILES,)),
            dma((TILES,)), dma((TILES,)),
            dma((TILES,)), dma((TILES,)),
            dma((1,)), dma((1,)),
            dma((10,)), dma((10,)),
            dma((TILES,)), dma((TILES,)),
            dma((6,)),
            dma((2 * TILES,)),
        ],
        compiler_params=pltpu.CompilerParams(
            collective_id=0, has_side_effects=True, vmem_limit_bytes=(53 << 20) + (256 << 10)
        ),
    )(
        block_target.reshape(K),
        block_source.reshape(K),
        block_count,
        features.reshape(tiles),
        hop_noise.reshape((2,) + tiles),
        encoder_weight,
        tile_mask[0],
    )
    return one.reshape(features.shape), two.reshape(features.shape)


def solution(mesh):
    in_specs = (
        P("blk", "feat"),
        P(None, "blk", "feat"),
        P(),
        P("blk", None),
        P("blk", None),
        P("blk"),
        P("blk", None, None, None),
    )
    out_specs = (P("blk", "feat"), P("blk", "feat"))
    return jax.shard_map(
        per_device, mesh=mesh, in_specs=in_specs, out_specs=out_specs, check_vma=False
    )
```

```python
import jax
import jax.numpy as jnp
from jax import lax
from jax.experimental import pallas as pl
from jax.experimental.pallas import tpu as pltpu
from jax.sharding import PartitionSpec as P

TILE = 128
TILES = 8
K = 40
Q = 4
QB = TILES // Q
EARLY = 3
LATE_AT = 7
WINDOW = 4
DRIP = 2
MID = 0
UNROLL = 10
ELAG = 1
LAG = 3
MESH = pl.DeviceIdType.MESH
F32 = jnp.float32
BF16 = jnp.bfloat16
PERM, SRC, KEEP, LAST, HAS = range(5)


class Links:
    def __init__(self, sems):
        self.sems = sems
        self.started = []
        self.known = {}
        self.arrived = set()

    def go(self, name, index, src, dst, device, lands=None, when=None):
        send, recv = self.sems[name]
        lands = index if lands is None else lands
        copy = pltpu.make_async_remote_copy(
            src_ref=src, dst_ref=dst, send_sem=send.at[index], recv_sem=recv.at[lands],
            device_id=device, device_id_type=MESH,
        )
        if when is None:
            copy.start()
        else:
            pl.when(when)(copy.start)
        self.started.append((copy, when, (name, index)))
        self.known[name, lands] = copy

    def sent(self, name, index):
        for i, (copy, when, at) in enumerate(self.started):
            if at == (name, index):
                copy.wait_send()
                del self.started[i]
                return

    def arrive(self, name, index):
        self.known[name, index].wait_recv()
        self.arrived.add((name, index))

    def finish(self):
        for copy, when, _ in self.started:
            if when is None:
                copy.wait_send()
            else:
                pl.when(when)(copy.wait_send)
        for at, copy in self.known.items():
            if at not in self.arrived:
                copy.wait_recv()


def list_order(targets, sources, count):
    spot_of = lax.broadcasted_iota(jnp.int32, (K, TILE), 0)
    lane = lax.broadcasted_iota(jnp.int32, (K, TILE), 1)
    same = spot_of == lane
    key = jnp.where(lane[:1] < count, targets, TILES) * 64 + lane[:1]

    def down(row):
        return jnp.sum(jnp.where(same, row, 0), axis=1, keepdims=True)

    def across(values, there):
        return jnp.sum(jnp.where(there, values, 0), axis=0, keepdims=True)

    key_down, source_down, target_down = down(key), down(sources), down(jnp.where(lane[:1] < count, targets, TILES))
    rank = jnp.sum(jnp.where((lane < K) & (key < key_down), 1, 0), axis=1, keepdims=True)
    at = rank == lane
    now = across(target_down, at)
    before = across(target_down, rank == lane - 1)
    keep = jnp.where((now == before) & (lane[:1] > 0), 1, 0)
    last = jnp.maximum(across(1, key_down < (lane + 1) * 64) - 1, 0)
    has = jnp.minimum(across(1, target_down == lane), 1)
    return across(spot_of, at), across(source_down, at), keep, last, has


def kernel(
    lists, feat, noise, weight, mask, out_one, out_two,
    info, order, win0, win1, masks_in, masks, weights, noises, noisy, sums, squares, chips, scales,
    encoded, own_one, own_two, noisy_two, others, partial,
    halo0_s, halo0_r, halo1_s, halo1_r, z_s, z_r, core_s, core_r, fwd_s, fwd_r,
    noise_s, noise_r, sq_s, sq_r, sc_s, sc_r, swap_s, swap_r, local, out_sem,
):
    parts = lax.axis_size("blk")
    b = lax.axis_index("blk")
    f = lax.axis_index("feat")
    zh = lax.div(f, 2)
    core = lax.rem(f, 2)
    fz = lax.rem(f + 2, 4)
    fc = f + 1 - 2 * core
    fd = lax.rem(fc + 2, 4)
    row_at = lax.rem(b, 32)
    x = lax.rem(b, 4)
    low, high = x < 2, x >= 2

    def at(by):
        return lax.rem(b + by + parts, parts)

    def half_at(by):
        crosses = row_at + by >= 32 if by > 0 else row_at + by < 0
        return jnp.where(crosses, fz, f)

    def dev(blk, col):
        return {"blk": blk, "feat": col}

    links = Links({
        "halo0": (halo0_s, halo0_r), "halo1": (halo1_s, halo1_r), "z": (z_s, z_r),
        "core": (core_s, core_r), "fwd": (fwd_s, fwd_r), "noise": (noise_s, noise_r),
        "sq": (sq_s, sq_r), "sc": (sc_s, sc_r), "swap": (swap_s, swap_r),
    })
    go, arrive = links.go, links.arrive
    outs = []

    loads = [
        pltpu.make_async_copy(feat, win0.at[pl.ds(16, 8)], local.at[0]),
        pltpu.make_async_copy(mask, masks_in, local.at[1]),
        pltpu.make_async_copy(noise.at[0], noises.at[2], local.at[2]),
        pltpu.make_async_copy(noise.at[1], noises.at[zh], local.at[3]),
        pltpu.make_async_copy(weight, weights, local.at[4]),
    ]
    loaded = set()
    for copy in loads:
        copy.start()

    def load(i):
        loads[i].wait()
        loaded.add(i)

    def finish():
        links.finish()
        for i in range(5):
            if i not in loaded:
                loads[i].wait()
        for copy in outs:
            copy.wait()

    barrier = pltpu.get_barrier_semaphore()
    met = [dev(at(by), col) for by in (1, -1, 2, -2, 3, -3) for col in (f, fz)] + [dev(b, fz), dev(b, fc)]
    for device in met:
        pl.semaphore_signal(barrier, inc=1, device_id=device, device_id_type=MESH)

    ones = jnp.ones((8, TILE), F32)
    for t in range(TILES):
        wide = feat[t].astype(F32)
        row = lax.dot_general(
            ones, wide * wide, (((1,), (1,)), ((), ())),
            precision=lax.Precision.HIGHEST, preferred_element_type=F32,
        )
        squares[0, t : t + 1, :] = row[0:1, :]
    lanes = lax.broadcasted_iota(jnp.int32, (1, TILE), 1)
    target_row = source_row = jnp.zeros((1, TILE), jnp.int32)
    for k in range(K):
        target_row = jnp.where(lanes == k, lists[k], target_row)
        source_row = jnp.where(lanes == k, lists[K + k], source_row)
    order[...] = jnp.zeros((8, TILE), jnp.int32)
    for i, row in enumerate(list_order(target_row, source_row, lists[2 * K])):
        order[i : i + 1, :] = row
    listed = pltpu.make_async_copy(order, info, local.at[5])
    listed.start()
    listed.wait()
    load(1)

    def take_mask(k, carry):
        masks[k] = masks_in[info[PERM, k]].astype(F32).astype(BF16)
        return carry

    lax.fori_loop(0, K, take_mask, 0)
    pl.semaphore_wait(barrier, len(met))

    class Halo:
        def __init__(self, name, WINDOW, count, size, half):
            self.name, self.window, self.count, self.size, self.half = name, WINDOW, count, size, half

        def part(self, block, q):
            return self.window.at[pl.ds(block + q * self.size, self.size)]

        def go(self, kind, q, src, slot, by, when=None):
            lands = {8: 0, 24: 1, 0: 2, 32: 3}[slot]
            go(
                self.name, kind * self.count + q, src, self.part(slot, q), dev(at(by), self.half(by)),
                lands * self.count + q, when,
            )

        def own(self, q, src=None):
            src = self.part(16, q) if src is None else src
            self.go(0, q, src, 8, 1)
            self.go(1, q, src, 24, -1)

        def far(self, q):
            for kind, (below, above) in enumerate(((3, -3), (1, -1))):
                @pl.when(low)
                def _():
                    arrive(self.name, (1 - kind) * self.count + q)

                self.go(2 + kind, q, self.part((24, 8)[kind], q), 0, below, low)

                @pl.when(high)
                def _():
                    arrive(self.name, kind * self.count + q)

                self.go(4 + kind, q, self.part((8, 24)[kind], q), 32, above, high)

        def last(self, q):
            arrive(self.name, 2 * self.count + q)
            arrive(self.name, 3 * self.count + q)

    raw = Halo("halo0", win0, Q, QB, lambda by: f)
    clipped = Halo("halo1", win1, TILES, 1, half_at)
    go("sq", 0, squares.at[0], squares.at[1], dev(b, fc))
    for q in range(Q):
        raw.own(q, feat.at[pl.ds(q * QB, QB)])
    arrive("sq", 0)
    mine_now = pl.ds(16, 8)
    chips[zh, mine_now, :] = squares[0] + squares[1]
    for i, by in enumerate((0, 1, -1, 2, -2)):
        there = pl.ds(16 - 8 * by, 8)
        go("sc", 2 * i, chips.at[zh, mine_now], chips.at[zh, there], dev(at(by), fz))
        if by:
            go("sc", 2 * i + 1, chips.at[zh, mine_now], chips.at[zh, there], dev(at(by), f))

    def send_noise(t):
        go("noise", t, noise.at[1, t], noises.at[zh, t], dev(b, fz))

    for t in range(EARLY):
        send_noise(t)

    for q in range(Q):
        raw.far(q)
    load(0)
    for i in range(10):
        if i != 1:
            arrive("sc", i)
    scales[...] = 1.0 / jnp.maximum(1.0, jnp.sqrt(chips[0] + chips[1]))
    for q in range(Q):
        raw.last(q)

    for t in range(EARLY, EARLY + MID):
        send_noise(t)

    def add_up(width, left, right):
        def step(i, acc):
            for u in range(UNROLL):
                k = i * UNROLL + u
                keep = info[KEEP, k].astype(F32)
                acc = acc * keep + jnp.dot(left(k), right(k), preferred_element_type=F32)
                sums[k, :, 0:width] = acc
            return acc

        lax.fori_loop(0, K // UNROLL, step, jnp.zeros((TILE, width), F32))

    def scaled_mask(k):
        row = scales[pl.ds(info[SRC, k], 1), :]
        return (masks[k].astype(F32) * row).astype(BF16)

    add_up(TILE, scaled_mask, lambda k: win0[info[SRC, k]])

    load(2)

    def send_z(t):
        go("z", t, noisy.at[f, t], noisy.at[f, t], dev(b, fz))

    for t in range(TILES):
        has = info[HAS, t].astype(F32)
        rows = sums[info[LAST, t], :, 0:TILE] * has
        noisy[f, t] = (rows + noises[2, t].astype(F32)).astype(BF16)
        if t < WINDOW:
            send_z(t)
        go("core", t, noisy.at[f, t], noisy.at[f, t], dev(b, fc))

    load(4)

    def encode(t):
        arrive("core", t)
        arrive("fwd", t)
        left = jnp.concatenate([noisy[g, t] for g in range(4)], axis=1)
        rounded = jnp.dot(left, weights[0], preferred_element_type=F32).astype(BF16)
        wide = rounded.astype(F32)
        norm = jnp.sqrt(jnp.sum(wide * wide, axis=1, keepdims=True))
        inverse = 1.0 / jnp.maximum(1.0, norm)
        for g in range(4):
            encoded[g] = rounded[:, g * TILE : (g + 1) * TILE]
        own_one[t] = encoded[f]
        for half in range(2):
            win1[16 + t, half] = (encoded[half * 2 + core].astype(F32) * inverse).astype(BF16)
        clipped.own(t)
        copy = pltpu.make_async_copy(own_one.at[t], out_one.at[t], out_sem.at[t])
        copy.start()
        outs.append(copy)

    for t in range(TILES + LAG + ELAG):
        if t < TILES:
            if t + WINDOW < TILES:
                links.sent("z", t)
                send_z(t + WINDOW)
            arrive("z", t)
            go("fwd", t, noisy.at[fz, t], noisy.at[fz, t], dev(b, fc))
        if 0 <= t - ELAG < TILES:
            encode(t - ELAG)
        if t >= LATE_AT:
            sent = EARLY + MID + (t - LATE_AT) * DRIP
            for late in range(sent, min(TILES, sent + DRIP)):
                send_noise(late)
        if 0 <= t - LAG - ELAG < TILES:
            clipped.far(t - LAG - ELAG)

    for t in range(TILES):
        clipped.last(t)

    add_up(
        2 * TILE,
        lambda k: masks[k],
        lambda k: jnp.concatenate([win1[info[SRC, k], 0], win1[info[SRC, k], 1]], axis=1),
    )

    load(3)
    mine = pl.ds(pl.multiple_of(f * TILE, TILE), TILE)
    upper = pl.multiple_of(core * TILE, TILE)
    other = pl.multiple_of(TILE - core * TILE, TILE)

    def columns_of(start):
        return jnp.concatenate([weights[1, pl.ds(row, TILE), mine] for row in (start, start + 2 * TILE)], axis=0)

    for t in range(TILES):
        arrive("noise", t)
        has = info[HAS, t].astype(F32)
        rows = sums[info[LAST, t]] * has
        for half in range(2):
            noisy_two[t, half] = (
                rows[:, half * TILE : (half + 1) * TILE] + noises[half, t].astype(F32)
            ).astype(BF16)
        go("swap", t, noisy_two.at[t], others.at[t], dev(b, fc))

    for t in range(TILES):
        left = jnp.concatenate([noisy_two[t, 0], noisy_two[t, 1]], axis=1)
        partial[t] = jnp.dot(left, columns_of(upper), preferred_element_type=F32)
    for t in range(TILES):
        arrive("swap", t)
        left = jnp.concatenate([others[t, 0], others[t, 1]], axis=1)
        rest = jnp.dot(left, columns_of(other), preferred_element_type=F32)
        own_two[t] = (partial[t] + rest).astype(BF16)
        copy = pltpu.make_async_copy(own_two.at[t], out_two.at[t], out_sem.at[TILES + t])
        copy.start()
        outs.append(copy)
    finish()


def per_device(
    features, hop_noise, encoder_weight, block_target, block_source, block_count, tile_mask
):
    tiles = (TILES, TILE, TILE)
    dma = pltpu.SemaphoreType.DMA
    anywhere = pl.BlockSpec(memory_space=pl.ANY)
    one, two = pl.pallas_call(
        kernel,
        out_shape=[jax.ShapeDtypeStruct(tiles, BF16)] * 2,
        in_specs=[
            pl.BlockSpec(memory_space=pltpu.SMEM),
            pl.BlockSpec(memory_space=pltpu.VMEM),
            anywhere, anywhere, anywhere,
        ],
        out_specs=[anywhere, anywhere],
        scratch_shapes=[
            pltpu.SMEM((8, TILE), jnp.int32),
            pltpu.VMEM((8, TILE), jnp.int32),
            pltpu.VMEM((K, TILE, TILE), BF16),
            pltpu.VMEM((K, 2, TILE, TILE), BF16),
            pltpu.VMEM((K, TILE, TILE), jnp.int32),
            pltpu.VMEM((K, TILE, TILE), BF16),
            pltpu.VMEM((2, 512, 512), BF16),
            pltpu.VMEM((3,) + tiles, BF16),
            pltpu.VMEM((4,) + tiles, BF16),
            pltpu.VMEM((K, TILE, 2 * TILE), F32),
            pltpu.VMEM((2, TILES, TILE), F32),
            pltpu.VMEM((2, K, TILE), F32),
            pltpu.VMEM((K, TILE), F32),
            pltpu.VMEM((4, TILE, TILE), BF16),
            pltpu.VMEM(tiles, BF16),
            pltpu.VMEM(tiles, BF16),
            pltpu.VMEM((TILES, 2, TILE, TILE), BF16),
            pltpu.VMEM((TILES, 2, TILE, TILE), BF16),
            pltpu.VMEM(tiles, F32),
            dma((6 * TILES,)), dma((4 * TILES,)),
            dma((6 * TILES,)), dma((4 * TILES,)),
            dma((TILES,)), dma((TILES,)),
            dma((TILES,)), dma((TILES,)),
            dma((TILES,)), dma((TILES,)),
            dma((TILES,)), dma((TILES,)),
            dma((1,)), dma((1,)),
            dma((10,)), dma((10,)),
            dma((TILES,)), dma((TILES,)),
            dma((6,)),
            dma((2 * TILES,)),
        ],
        compiler_params=pltpu.CompilerParams(
            collective_id=0, has_side_effects=True, vmem_limit_bytes=(53 << 20) + (256 << 10)
        ),
    )(
        jnp.concatenate([block_target[0], block_source[0], block_count]),
        features.reshape(tiles),
        hop_noise.reshape((2,) + tiles),
        encoder_weight,
        tile_mask[0],
    )
    return one.reshape(features.shape), two.reshape(features.shape)


def solution(mesh):
    in_specs = (
        P("blk", "feat"),
        P(None, "blk", "feat"),
        P(),
        P("blk", None),
        P("blk", None),
        P("blk"),
        P("blk", None, None, None),
    )
    out_specs = (P("blk", "feat"), P("blk", "feat"))
    return jax.shard_map(
        per_device, mesh=mesh, in_specs=in_specs, out_specs=out_specs, check_vma=False
    )
```

```python
import jax
import jax.numpy as jnp
from jax import lax
from jax.experimental import pallas as pl
from jax.experimental.pallas import tpu as pltpu
from jax.sharding import PartitionSpec as P

TILE = 128
TILES = 8
K = 40
Q = 4
QB = TILES // Q
EARLY = 3
LATE_AT = 7
WINDOW = 4
DRIP = 2
MID = 0
UNROLL = 10
ELAG = 1
LAG = 3
MESH = pl.DeviceIdType.MESH
F32 = jnp.float32
BF16 = jnp.bfloat16
PERM, SRC, KEEP, LAST, HAS = range(5)


class Links:
    def __init__(self, sems):
        self.sems = sems
        self.started = []
        self.known = {}
        self.arrived = set()

    def go(self, name, index, src, dst, device, lands=None, when=None):
        send, recv = self.sems[name]
        lands = index if lands is None else lands
        copy = pltpu.make_async_remote_copy(
            src_ref=src, dst_ref=dst, send_sem=send.at[index], recv_sem=recv.at[lands],
            device_id=device, device_id_type=MESH,
        )
        if when is None:
            copy.start()
        else:
            pl.when(when)(copy.start)
        self.started.append((copy, when, (name, index)))
        self.known[name, lands] = copy

    def sent(self, name, index):
        for i, (copy, when, at) in enumerate(self.started):
            if at == (name, index):
                copy.wait_send()
                del self.started[i]
                return

    def arrive(self, name, index):
        self.known[name, index].wait_recv()
        self.arrived.add((name, index))

    def finish(self):
        for copy, when, _ in self.started:
            if when is None:
                copy.wait_send()
            else:
                pl.when(when)(copy.wait_send)
        for at, copy in self.known.items():
            if at not in self.arrived:
                copy.wait_recv()


def list_order(targets, sources, count):
    spot_of = lax.broadcasted_iota(jnp.int32, (K, TILE), 0)
    lane = lax.broadcasted_iota(jnp.int32, (K, TILE), 1)
    same = spot_of == lane
    key = jnp.where(lane[:1] < count, targets, TILES) * 64 + lane[:1]

    def down(row):
        return jnp.sum(jnp.where(same, row, 0), axis=1, keepdims=True)

    def across(values, there):
        return jnp.sum(jnp.where(there, values, 0), axis=0, keepdims=True)

    key_down, source_down, target_down = down(key), down(sources), down(jnp.where(lane[:1] < count, targets, TILES))
    rank = jnp.sum(jnp.where((lane < K) & (key < key_down), 1, 0), axis=1, keepdims=True)
    at = rank == lane
    now = across(target_down, at)
    before = across(target_down, rank == lane - 1)
    keep = jnp.where((now == before) & (lane[:1] > 0), 1, 0)
    last = jnp.maximum(across(1, key_down < (lane + 1) * 64) - 1, 0)
    has = jnp.minimum(across(1, target_down == lane), 1)
    return across(spot_of, at), across(source_down, at), keep, last, has


def kernel(
    lists, feat, noise, weight, mask, out_one, out_two,
    info, order, win0, win1, masks_in, masks, weights, noises, noisy, sums, squares, chips, scales,
    encoded, own_one, own_two, noisy_two, others, partial,
    halo0_s, halo0_r, halo1_s, halo1_r, z_s, z_r, core_s, core_r, fwd_s, fwd_r,
    noise_s, noise_r, sq_s, sq_r, sc_s, sc_r, swap_s, swap_r, local, out_sem,
):
    parts = lax.axis_size("blk")
    b = lax.axis_index("blk")
    f = lax.axis_index("feat")
    zh = lax.div(f, 2)
    core = lax.rem(f, 2)
    fz = lax.rem(f + 2, 4)
    fc = f + 1 - 2 * core
    fd = lax.rem(fc + 2, 4)
    row_at = lax.rem(b, 32)
    x = lax.rem(b, 4)
    low, high = x < 2, x >= 2

    def at(by):
        return lax.rem(b + by + parts, parts)

    def half_at(by):
        crosses = row_at + by >= 32 if by > 0 else row_at + by < 0
        return jnp.where(crosses, fz, f)

    def dev(blk, col):
        return {"blk": blk, "feat": col}

    links = Links({
        "halo0": (halo0_s, halo0_r), "halo1": (halo1_s, halo1_r), "z": (z_s, z_r),
        "core": (core_s, core_r), "fwd": (fwd_s, fwd_r), "noise": (noise_s, noise_r),
        "sq": (sq_s, sq_r), "sc": (sc_s, sc_r), "swap": (swap_s, swap_r),
    })
    go, arrive = links.go, links.arrive
    outs = []

    loads = [
        pltpu.make_async_copy(feat, win0.at[pl.ds(16, 8)], local.at[0]),
        pltpu.make_async_copy(mask, masks_in, local.at[1]),
        pltpu.make_async_copy(noise.at[0], noises.at[2], local.at[2]),
        pltpu.make_async_copy(noise.at[1], noises.at[zh], local.at[3]),
        pltpu.make_async_copy(weight, weights, local.at[4]),
    ]
    loaded = set()
    for copy in loads:
        copy.start()

    def load(i):
        loads[i].wait()
        loaded.add(i)

    def finish():
        links.finish()
        for i in range(5):
            if i not in loaded:
                loads[i].wait()
        for copy in outs:
            copy.wait()

    barrier = pltpu.get_barrier_semaphore()
    met = [dev(at(by), col) for by in (1, -1, 2, -2, 3, -3) for col in (f, fz)] + [dev(b, fz), dev(b, fc)]
    for device in met:
        pl.semaphore_signal(barrier, inc=1, device_id=device, device_id_type=MESH)

    for t in range(TILES):
        wide = feat[t].astype(F32)
        squares[0, t : t + 1, :] = jnp.sum((wide * wide).T, axis=0, keepdims=True)
    lanes = lax.broadcasted_iota(jnp.int32, (1, TILE), 1)
    target_row = source_row = jnp.zeros((1, TILE), jnp.int32)
    for k in range(K):
        target_row = jnp.where(lanes == k, lists[k], target_row)
        source_row = jnp.where(lanes == k, lists[K + k], source_row)
    order[...] = jnp.zeros((8, TILE), jnp.int32)
    for i, row in enumerate(list_order(target_row, source_row, lists[2 * K])):
        order[i : i + 1, :] = row
    listed = pltpu.make_async_copy(order, info, local.at[5])
    listed.start()
    listed.wait()
    load(1)

    def take_mask(k, carry):
        masks[k] = masks_in[info[PERM, k]].astype(F32).astype(BF16)
        return carry

    lax.fori_loop(0, K, take_mask, 0)
    pl.semaphore_wait(barrier, len(met))

    class Halo:
        def __init__(self, name, WINDOW, count, size, half):
            self.name, self.window, self.count, self.size, self.half = name, WINDOW, count, size, half

        def part(self, block, q):
            return self.window.at[pl.ds(block + q * self.size, self.size)]

        def go(self, kind, q, src, slot, by, when=None):
            lands = {8: 0, 24: 1, 0: 2, 32: 3}[slot]
            go(
                self.name, kind * self.count + q, src, self.part(slot, q), dev(at(by), self.half(by)),
                lands * self.count + q, when,
            )

        def own(self, q, src=None):
            src = self.part(16, q) if src is None else src
            self.go(0, q, src, 8, 1)
            self.go(1, q, src, 24, -1)

        def far(self, q):
            for kind, (below, above) in enumerate(((3, -3), (1, -1))):
                @pl.when(low)
                def _():
                    arrive(self.name, (1 - kind) * self.count + q)

                self.go(2 + kind, q, self.part((24, 8)[kind], q), 0, below, low)

                @pl.when(high)
                def _():
                    arrive(self.name, kind * self.count + q)

                self.go(4 + kind, q, self.part((8, 24)[kind], q), 32, above, high)

        def last(self, q):
            arrive(self.name, 2 * self.count + q)
            arrive(self.name, 3 * self.count + q)

    raw = Halo("halo0", win0, Q, QB, lambda by: f)
    clipped = Halo("halo1", win1, TILES, 1, half_at)
    go("sq", 0, squares.at[0], squares.at[1], dev(b, fc))
    for q in range(Q):
        raw.own(q, feat.at[pl.ds(q * QB, QB)])
    arrive("sq", 0)
    mine_now = pl.ds(16, 8)
    chips[zh, mine_now, :] = squares[0] + squares[1]
    for i, by in enumerate((0, 1, -1, 2, -2)):
        there = pl.ds(16 - 8 * by, 8)
        go("sc", 2 * i, chips.at[zh, mine_now], chips.at[zh, there], dev(at(by), fz))
        if by:
            go("sc", 2 * i + 1, chips.at[zh, mine_now], chips.at[zh, there], dev(at(by), f))

    def send_noise(t):
        go("noise", t, noise.at[1, t], noises.at[zh, t], dev(b, fz))

    for t in range(EARLY):
        send_noise(t)

    for q in range(Q):
        raw.far(q)
    load(0)
    for i in range(10):
        if i != 1:
            arrive("sc", i)
    scales[...] = 1.0 / jnp.maximum(1.0, jnp.sqrt(chips[0] + chips[1]))
    for q in range(Q):
        raw.last(q)

    for t in range(EARLY, EARLY + MID):
        send_noise(t)

    def add_up(width, left, right):
        def step(i, acc):
            for u in range(UNROLL):
                k = i * UNROLL + u
                keep = info[KEEP, k].astype(F32)
                acc = acc * keep + jnp.dot(left(k), right(k), preferred_element_type=F32)
                sums[k, :, 0:width] = acc
            return acc

        lax.fori_loop(0, K // UNROLL, step, jnp.zeros((TILE, width), F32))

    def scaled_mask(k):
        row = scales[pl.ds(info[SRC, k], 1), :]
        return (masks[k].astype(F32) * row).astype(BF16)

    add_up(TILE, scaled_mask, lambda k: win0[info[SRC, k]])

    load(2)

    def send_z(t):
        go("z", t, noisy.at[f, t], noisy.at[f, t], dev(b, fz))

    for t in range(TILES):
        has = info[HAS, t].astype(F32)
        rows = sums[info[LAST, t], :, 0:TILE] * has
        noisy[f, t] = (rows + noises[2, t].astype(F32)).astype(BF16)
        if t < WINDOW:
            send_z(t)
        go("core", t, noisy.at[f, t], noisy.at[f, t], dev(b, fc))

    load(4)

    def encode(t):
        arrive("core", t)
        arrive("fwd", t)
        left = jnp.concatenate([noisy[g, t] for g in range(4)], axis=1)
        rounded = jnp.dot(left, weights[0], preferred_element_type=F32).astype(BF16)
        wide = rounded.astype(F32)
        norm = jnp.sqrt(jnp.sum(wide * wide, axis=1, keepdims=True))
        inverse = 1.0 / jnp.maximum(1.0, norm)
        for g in range(4):
            encoded[g] = rounded[:, g * TILE : (g + 1) * TILE]
        own_one[t] = encoded[f]
        for half in range(2):
            win1[16 + t, half] = (encoded[half * 2 + core].astype(F32) * inverse).astype(BF16)
        clipped.own(t)
        copy = pltpu.make_async_copy(own_one.at[t], out_one.at[t], out_sem.at[t])
        copy.start()
        outs.append(copy)

    for t in range(TILES + LAG + ELAG):
        if t < TILES:
            if t + WINDOW < TILES:
                links.sent("z", t)
                send_z(t + WINDOW)
            arrive("z", t)
            go("fwd", t, noisy.at[fz, t], noisy.at[fz, t], dev(b, fc))
        if 0 <= t - ELAG < TILES:
            encode(t - ELAG)
        if t >= LATE_AT:
            sent = EARLY + MID + (t - LATE_AT) * DRIP
            for late in range(sent, min(TILES, sent + DRIP)):
                send_noise(late)
        if 0 <= t - LAG - ELAG < TILES:
            clipped.far(t - LAG - ELAG)

    for t in range(TILES):
        clipped.last(t)

    add_up(
        2 * TILE,
        lambda k: masks[k],
        lambda k: jnp.concatenate([win1[info[SRC, k], 0], win1[info[SRC, k], 1]], axis=1),
    )

    load(3)
    mine = pl.ds(pl.multiple_of(f * TILE, TILE), TILE)
    upper = pl.multiple_of(core * TILE, TILE)
    other = pl.multiple_of(TILE - core * TILE, TILE)

    def columns_of(start):
        return jnp.concatenate([weights[1, pl.ds(row, TILE), mine] for row in (start, start + 2 * TILE)], axis=0)

    for t in range(TILES):
        arrive("noise", t)
        has = info[HAS, t].astype(F32)
        rows = sums[info[LAST, t]] * has
        for half in range(2):
            noisy_two[t, half] = (
                rows[:, half * TILE : (half + 1) * TILE] + noises[half, t].astype(F32)
            ).astype(BF16)
        go("swap", t, noisy_two.at[t], others.at[t], dev(b, fc))

    for t in range(TILES):
        left = jnp.concatenate([noisy_two[t, 0], noisy_two[t, 1]], axis=1)
        partial[t] = jnp.dot(left, columns_of(upper), preferred_element_type=F32)
    for t in range(TILES):
        arrive("swap", t)
        left = jnp.concatenate([others[t, 0], others[t, 1]], axis=1)
        rest = jnp.dot(left, columns_of(other), preferred_element_type=F32)
        own_two[t] = (partial[t] + rest).astype(BF16)
        copy = pltpu.make_async_copy(own_two.at[t], out_two.at[t], out_sem.at[TILES + t])
        copy.start()
        outs.append(copy)
    finish()


def per_device(
    features, hop_noise, encoder_weight, block_target, block_source, block_count, tile_mask
):
    tiles = (TILES, TILE, TILE)
    dma = pltpu.SemaphoreType.DMA
    anywhere = pl.BlockSpec(memory_space=pl.ANY)
    one, two = pl.pallas_call(
        kernel,
        out_shape=[jax.ShapeDtypeStruct(tiles, BF16)] * 2,
        in_specs=[
            pl.BlockSpec(memory_space=pltpu.SMEM),
            pl.BlockSpec(memory_space=pltpu.VMEM),
            anywhere, anywhere, anywhere,
        ],
        out_specs=[anywhere, anywhere],
        scratch_shapes=[
            pltpu.SMEM((8, TILE), jnp.int32),
            pltpu.VMEM((8, TILE), jnp.int32),
            pltpu.VMEM((K, TILE, TILE), BF16),
            pltpu.VMEM((K, 2, TILE, TILE), BF16),
            pltpu.VMEM((K, TILE, TILE), jnp.int32),
            pltpu.VMEM((K, TILE, TILE), BF16),
            pltpu.VMEM((2, 512, 512), BF16),
            pltpu.VMEM((3,) + tiles, BF16),
            pltpu.VMEM((4,) + tiles, BF16),
            pltpu.VMEM((K, TILE, 2 * TILE), F32),
            pltpu.VMEM((2, TILES, TILE), F32),
            pltpu.VMEM((2, K, TILE), F32),
            pltpu.VMEM((K, TILE), F32),
            pltpu.VMEM((4, TILE, TILE), BF16),
            pltpu.VMEM(tiles, BF16),
            pltpu.VMEM(tiles, BF16),
            pltpu.VMEM((TILES, 2, TILE, TILE), BF16),
            pltpu.VMEM((TILES, 2, TILE, TILE), BF16),
            pltpu.VMEM(tiles, F32),
            dma((6 * TILES,)), dma((4 * TILES,)),
            dma((6 * TILES,)), dma((4 * TILES,)),
            dma((TILES,)), dma((TILES,)),
            dma((TILES,)), dma((TILES,)),
            dma((TILES,)), dma((TILES,)),
            dma((TILES,)), dma((TILES,)),
            dma((1,)), dma((1,)),
            dma((10,)), dma((10,)),
            dma((TILES,)), dma((TILES,)),
            dma((6,)),
            dma((2 * TILES,)),
        ],
        compiler_params=pltpu.CompilerParams(
            collective_id=0, has_side_effects=True, vmem_limit_bytes=(53 << 20) + (256 << 10)
        ),
    )(
        jnp.concatenate([block_target[0], block_source[0], block_count]),
        features.reshape(tiles),
        hop_noise.reshape((2,) + tiles),
        encoder_weight,
        tile_mask[0],
    )
    return one.reshape(features.shape), two.reshape(features.shape)


def solution(mesh):
    in_specs = (
        P("blk", "feat"),
        P(None, "blk", "feat"),
        P(),
        P("blk", None),
        P("blk", None),
        P("blk"),
        P("blk", None, None, None),
    )
    out_specs = (P("blk", "feat"), P("blk", "feat"))
    return jax.shard_map(
        per_device, mesh=mesh, in_specs=in_specs, out_specs=out_specs, check_vma=False
    )
```
